512 devices in a mesh: fsdp: 64 (over z, y), tp: 8 (over x, core).
Axes of the slice: x: 4, y: 8, z: 8, core: 2. Of those that a mesh axis runs over, the one named last changes fastest.
Arguments:
- momentum: bfloat16 [8192, 26624], P('fsdp', 'tp'), may hold values from -6 to 6
- gradient: bfloat16 [8192, 26624], P('fsdp', 'tp'), may hold values from -150 to 150
- right_factor: bfloat16 [256, 26624], P('fsdp', 'tp'), may hold values from -0.0390625 to 0.0390625
Outputs:
- momentum_next: bfloat16 [8192, 26624], P('fsdp', 'tp')
- factor_next: float32 [256, 26624], P('fsdp', 'tp')
- update: bfloat16 [8192, 26624], P('fsdp', 'tp')
The draws below stay inside these ranges and needn't reach their ends.
All inputs are finite; a program needn't handle non-finite values.
Results may differ from the reference program's by a relative error of at most 0.012.
Values may be sent and summed in bfloat16 or wider, within the bound.
No kernel may reach another device: no remote copies, remote signals or barrier semaphores. Data moves between devices by JAX's collectives and lax.ppermute only.
A program may use at most 64 MiB of HBM per device.

```python
import math
import jax
import jax.numpy as jnp
from jax import lax

N = 26624
RANK = 256
M_ROWS = 8192


def draw_gradient(key, part):
    key = jax.random.fold_in(key, 7)
    base_key, row_key, col_key = jax.random.split(key, 3)
    positions = jnp.arange(N, dtype=jnp.float32)[None, :] / N
    values = jnp.clip(jax.random.normal(base_key, (M_ROWS, N), jnp.float32), -4.0, 4.0)
    row_scale = jnp.exp(jax.random.uniform(row_key, (M_ROWS, 1), jnp.float32) * math.log(10.0))
    col_scale = jnp.exp(jax.random.uniform(col_key, (1, N), jnp.float32) * math.log(4.0)) * jnp.exp(math.log(3.0) * positions)
    return jnp.clip(0.3 * values * row_scale * col_scale, -150.0, 150.0).astype(jnp.bfloat16)


def shard_levels(key, dims, cuts, least, largest):
    factor_of, own = 1.0, jax.random.fold_in(key, 6)
    for dim, parts in cuts:
        steps = jnp.exp(jax.random.uniform(jax.random.fold_in(own, dim), (parts,), jnp.float32, least / len(cuts), largest / len(cuts)))
        factor_of = factor_of * jnp.repeat(steps, dims[dim] // parts).reshape([-1 if axis == dim else 1 for axis in range(len(dims))])
    return factor_of


def bell_draw(rng, extent, scale, bound, cuts=(), held_as=jnp.bfloat16):
    gain = shard_levels(rng, extent, cuts, -0.22, 0.18) if cuts else 1.0
    result = jax.random.normal(rng, extent, jnp.float32) * scale * gain
    return jnp.minimum(jnp.maximum(result, -bound), bound).astype(held_as)


def setup_inputs(seed: int = 0) -> dict:
    arg_keys = jax.random.split(jax.random.key(seed), 4)
    return {
        "momentum": bell_draw(arg_keys[0], (M_ROWS, N), 1.0, 6.0, ((0, 64), (1, 8))),
        "gradient": draw_gradient(jax.random.fold_in(arg_keys[3], 71), 0),
        "right_factor": bell_draw(arg_keys[2], (RANK, N), N ** -0.5, 0.0390625, ((0, 64), (1, 8))),
    }


EPSILON = 1e-06
MOMENTUM_DECAY = 0.95

def reference(momentum, gradient, right_factor):
    blended = (momentum.astype(jnp.float32) + gradient.astype(jnp.float32)).astype(jnp.bfloat16)
    raw_basis = lax.dot_general(blended.astype(jnp.float32), right_factor.astype(jnp.float32), (((1,), (1,)), ((), ())), preferred_element_type=jnp.float32)
    gram_matrix = jnp.dot(raw_basis.T, raw_basis, precision=lax.Precision.HIGHEST)
    factor_lower = jnp.linalg.cholesky(gram_matrix)
    ortho_basis = lax.linalg.triangular_solve(factor_lower, raw_basis, left_side=False, lower=True, transpose_a=True).astype(jnp.bfloat16)
    projection = lax.dot_general(ortho_basis.astype(jnp.float32), blended.astype(jnp.float32), (((0,), (0,)), ((), ())), preferred_element_type=jnp.float32)
    col_norms = jnp.sqrt(lax.optimization_barrier(jnp.sum(projection * projection, axis=1, keepdims=True))) + EPSILON
    factor_next = projection / col_norms
    carried = jnp.dot(ortho_basis.astype(jnp.float32), projection.astype(jnp.bfloat16).astype(jnp.float32), preferred_element_type=jnp.float32)
    momentum_next = (blended.astype(jnp.float32) - (1.0 - MOMENTUM_DECAY) * carried).astype(jnp.bfloat16)
    scale_factor = math.sqrt(M_ROWS * N / RANK)
    direction = jnp.dot(ortho_basis.astype(jnp.float32), factor_next.astype(jnp.bfloat16).astype(jnp.float32), preferred_element_type=jnp.float32)
    update = (scale_factor * direction).astype(jnp.bfloat16)
    return (momentum_next, factor_next, update)
```

```python
import functools
import math

import jax
import jax.numpy as jnp
from jax import lax
from jax.experimental import pallas as pl
from jax.experimental.pallas import tpu as pltpu
from jax.sharding import Mesh, PartitionSpec as P

EPSILON = 1e-06
MOMENTUM_DECAY = 0.95
HIGHEST = lax.Precision.HIGHEST

ROWS_OVER = ("z", "y")
COLS_OVER = ("x", "core")
GRID = {"z": 8, "y": 8, "x": 4, "core": 2}
GROUPS = 64
CHUNK = 56

FACTOR_BLOCK = 64
FACTOR_GROUP = 8


def block_inverse(block, size):
    lane = lax.broadcasted_iota(jnp.int32, (size, 128), 1)
    sub = lax.broadcasted_iota(jnp.int32, (size, 128), 0)
    eye = (lane == sub + size).astype(jnp.float32)
    if 2 * size == 128:
        work = jnp.concatenate([block, jnp.zeros_like(block)], axis=1) + eye
    else:
        work = jnp.concatenate([block, jnp.zeros((size, 128 - size), jnp.float32)], axis=1) + eye
    pivots = jnp.ones((size, 128), jnp.float32)
    for start in range(0, size, FACTOR_GROUP):
        columns = [
            jnp.broadcast_to(work[:, j : j + 1], (size, 128))
            for j in range(start, start + FACTOR_GROUP)
        ]
        for c in range(FACTOR_GROUP):
            j = start + c
            pivot = jnp.broadcast_to(columns[c][j : j + 1, :], (size, 128))
            ratio = jnp.where(sub > j, columns[c] * (1.0 / pivot), 0.0)
            pivots = jnp.where(sub == j, pivot, pivots)
            work = work - ratio * jnp.broadcast_to(work[j : j + 1, :], (size, 128))
            for later in range(c + 1, FACTOR_GROUP):
                columns[later] = columns[later] - ratio * jnp.broadcast_to(
                    columns[later][j : j + 1, :], (size, 128)
                )
    work = work * lax.rsqrt(pivots)
    return work[:, size : 2 * size]


def factor_kernel(gram_ref, inverse_ref, *, size):
    inverse_ref[...] = gram_ref[...]
    step = FACTOR_BLOCK
    for k in range(0, size, step):
        after = k + step
        inverse = block_inverse(inverse_ref[k:after, k:after], step)
        panel = jnp.dot(
            inverse, inverse_ref[k:after, :], precision=HIGHEST, preferred_element_type=jnp.float32
        )
        pieces = [inverse]
        if k > 0:
            pieces = [panel[:, :k]] + pieces
        if after < size:
            pieces = pieces + [panel[:, after:]]
            lower = lax.dot_general(
                inverse_ref[after:, k:after],
                inverse,
                (((1,), (1,)), ((), ())),
                precision=HIGHEST,
                preferred_element_type=jnp.float32,
            )
        panel = jnp.concatenate(pieces, axis=1)
        inverse_ref[k:after, :] = panel
        if after < size:
            inverse_ref[after:, k:after] = jnp.zeros((size - after, step), jnp.float32)
            inverse_ref[after:, :] = inverse_ref[after:, :] - jnp.dot(
                lower, panel, precision=HIGHEST, preferred_element_type=jnp.float32
            )
    row = lax.broadcasted_iota(jnp.int32, (size, size), 0)
    col = lax.broadcasted_iota(jnp.int32, (size, size), 1)
    inverse_ref[...] = jnp.where(row >= col, inverse_ref[...], 0.0)


def inverse_factor(gram):
    size = gram.shape[0]
    return pl.pallas_call(
        functools.partial(factor_kernel, size=size),
        out_shape=jax.ShapeDtypeStruct((size, size), jnp.float32),
        in_specs=[pl.BlockSpec(memory_space=pltpu.VMEM)],
        out_specs=pl.BlockSpec(memory_space=pltpu.VMEM),
        compiler_params=pltpu.CompilerParams(vmem_limit_bytes=32 << 20),
        cost_estimate=pl.CostEstimate(flops=10**9, bytes_accessed=1 << 19, transcendentals=512),
        name="inverse_factor",
    )(gram)


def spread(block, axes, parts):
    copies = jnp.broadcast_to(block[None], (parts,) + block.shape)
    return lax.all_to_all(copies, axes, 0, 0, tiled=True)


def nt_dot(a, b, precision=None):
    return lax.dot_general(
        a, b, (((1,), (1,)), ((), ())), precision=precision, preferred_element_type=jnp.float32
    )


def body(momentum, gradient, right_factor):
    rows, cols = momentum.shape
    share_rank = right_factor.shape[0]
    rank = share_rank * GROUPS
    padded = GROUPS * CHUNK
    blended = (momentum.astype(jnp.float32) + gradient.astype(jnp.float32)).astype(jnp.bfloat16)
    with jax.named_scope("factor_gather"):
        whole_factor = spread(right_factor, ROWS_OVER, GROUPS).reshape(rank, cols)
    with jax.named_scope("basis"):
        basis = nt_dot(blended, whole_factor)
        basis = jnp.sum(spread(basis, "core", GRID["core"]), axis=0)
        basis = jnp.sum(spread(basis, "x", GRID["x"]), axis=0)
    with jax.named_scope("cross"):
        high = basis.astype(jnp.bfloat16)
        low = (basis - high.astype(jnp.float32)).astype(jnp.bfloat16)
        wide = jnp.pad(blended, ((0, 0), (0, padded - cols)))
        cross = lax.dot_general(
            jnp.concatenate([wide, wide], axis=0),
            jnp.concatenate([high, low], axis=0),
            (((0,), (0,)), ((), ())),
            preferred_element_type=jnp.float32,
        )
        cross = lax.psum_scatter(cross, "z", scatter_dimension=0, tiled=True)
    with jax.named_scope("gram"):
        gram = jnp.dot(basis.T, basis, precision=HIGHEST)
        gram = lax.all_to_all(
            gram.reshape(GROUPS, share_rank, rank), ROWS_OVER, 0, 0, tiled=True
        )
        gram = spread(jnp.sum(gram, axis=0), ROWS_OVER, GROUPS).reshape(rank, rank)
    with jax.named_scope("solve"):
        inverse = inverse_factor(gram)
        cross, inverse = lax.optimization_barrier((cross, inverse))
        ortho_basis = nt_dot(basis, inverse, HIGHEST).astype(jnp.bfloat16)
    with jax.named_scope("projection"):
        cross = lax.all_to_all(
            cross.reshape(GRID["y"], CHUNK, rank), "y", 0, 0, tiled=True
        )
        own = nt_dot(jnp.sum(cross, axis=0), inverse, HIGHEST).astype(jnp.bfloat16)
        projection = spread(own, ROWS_OVER, GROUPS).reshape(padded, rank)[:cols]
    with jax.named_scope("norms"):
        wide_proj = projection.astype(jnp.float32)
        squares = jnp.sum(wide_proj * wide_proj, axis=0)[None]
        squares = jnp.sum(spread(squares, COLS_OVER, GRID["x"] * GRID["core"]), axis=0)
        inverse_norms = 1.0 / (jnp.sqrt(squares) + EPSILON)
    with jax.named_scope("outputs"):
        carried = nt_dot(ortho_basis, projection)
        momentum_next = (blended.astype(jnp.float32) - (1.0 - MOMENTUM_DECAY) * carried).astype(
            jnp.bfloat16
        )
        scale_factor = math.sqrt(rows * GROUPS * cols * GRID["x"] * GRID["core"] / rank)
        scaled = (wide_proj * inverse_norms).astype(jnp.bfloat16)
        update = (scale_factor * nt_dot(ortho_basis, scaled)).astype(jnp.bfloat16)
        first = lax.axis_index(ROWS_OVER) * share_rank
        own_rank = first + lax.broadcasted_iota(jnp.int32, (share_rank, rank), 0)
        pick = own_rank == lax.broadcasted_iota(jnp.int32, (share_rank, rank), 1)
        own_norms = jnp.sum(jnp.where(pick, inverse_norms, 0.0), axis=1, keepdims=True)
        factor_next = nt_dot(pick.astype(jnp.bfloat16), projection) * own_norms
    return (momentum_next, factor_next, update)


def solution(mesh):
    chips = Mesh(mesh.devices.reshape(tuple(GRID.values())), tuple(GRID))
    placed = P(ROWS_OVER, COLS_OVER)
    return jax.shard_map(
        body,
        mesh=chips,
        in_specs=(placed, placed, placed),
        out_specs=(placed, placed, placed),
        check_vma=False,
    )
```

```python
import functools
import math

import jax
import jax.numpy as jnp
from jax import lax
from jax.experimental import pallas as pl
from jax.experimental.pallas import tpu as pltpu
from jax.sharding import PartitionSpec as P

EPSILON = 1e-06
MOMENTUM_DECAY = 0.95
HIGHEST = lax.Precision.HIGHEST

AXES = ("fsdp", "tp")
SIDE = 8
LINE = 4
CORES = 2


def groups_of(key, order):
    found = {}
    for index in range(SIDE * SIDE * LINE * CORES):
        fsdp, tp = divmod(index, LINE * CORES)
        place = divmod(fsdp, SIDE) + divmod(tp, CORES)
        found.setdefault(key(*place), []).append((order(*place), index))
    return [[index for _, index in sorted(group)] for group in found.values()]


def tile(place, core):
    return (place - core) % SIDE // 2


NEAR = groups_of(
    lambda z, y, x, core: (tile(z, core), tile(y, core), x, core), lambda z, y, x, core: (z % 2, y % 2)
)
STRIDED = groups_of(
    lambda z, y, x, core: (z % 2, y % 2, x, core), lambda z, y, x, core: (z // 2, y // 2)
)
MIDDLE = groups_of(
    lambda z, y, x, core: (z // 4, z % 2, y // 4, y % 2, x, core),
    lambda z, y, x, core: (z // 2, y // 2),
)
FAR = groups_of(lambda z, y, x, core: (z % 4, y % 4, x, core), lambda z, y, x, core: (z, y))
CHIP = groups_of(lambda z, y, x, core: (z, y, x), lambda z, y, x, core: core)
ROW = groups_of(lambda z, y, x, core: (z, y, core), lambda z, y, x, core: x)
COLUMNS = groups_of(lambda z, y, x, core: (z, y), lambda z, y, x, core: (x, core))

FACTOR_BLOCK = 64
FACTOR_GROUP = 8


def block_inverse(block, size):
    lane = lax.broadcasted_iota(jnp.int32, (size, 128), 1)
    sub = lax.broadcasted_iota(jnp.int32, (size, 128), 0)
    eye = (lane == sub + size).astype(jnp.float32)
    if 2 * size == 128:
        work = jnp.concatenate([block, jnp.zeros_like(block)], axis=1) + eye
    else:
        work = jnp.concatenate([block, jnp.zeros((size, 128 - size), jnp.float32)], axis=1) + eye
    pivots = jnp.ones((size, 128), jnp.float32)
    for start in range(0, size, FACTOR_GROUP):
        columns = [
            jnp.broadcast_to(work[:, j : j + 1], (size, 128))
            for j in range(start, start + FACTOR_GROUP)
        ]
        for c in range(FACTOR_GROUP):
            j = start + c
            pivot = jnp.broadcast_to(columns[c][j : j + 1, :], (size, 128))
            ratio = jnp.where(sub > j, columns[c] * (1.0 / pivot), 0.0)
            pivots = jnp.where(sub == j, pivot, pivots)
            work = work - ratio * jnp.broadcast_to(work[j : j + 1, :], (size, 128))
            for later in range(c + 1, FACTOR_GROUP):
                columns[later] = columns[later] - ratio * jnp.broadcast_to(
                    columns[later][j : j + 1, :], (size, 128)
                )
    work = work * lax.rsqrt(pivots)
    return work[:, size : 2 * size]


def factor_kernel(gram_ref, inverse_ref, *, size):
    inverse_ref[...] = gram_ref[...]
    step = FACTOR_BLOCK
    for k in range(0, size, step):
        after = k + step
        inverse = block_inverse(inverse_ref[k:after, k:after], step)
        panel = jnp.dot(
            inverse, inverse_ref[k:after, :], precision=HIGHEST, preferred_element_type=jnp.float32
        )
        pieces = [inverse]
        if k > 0:
            pieces = [panel[:, :k]] + pieces
        if after < size:
            pieces = pieces + [panel[:, after:]]
            lower = lax.dot_general(
                inverse_ref[after:, k:after],
                inverse,
                (((1,), (1,)), ((), ())),
                precision=HIGHEST,
                preferred_element_type=jnp.float32,
            )
        panel = jnp.concatenate(pieces, axis=1)
        inverse_ref[k:after, :] = panel
        if after < size:
            inverse_ref[after:, k:after] = jnp.zeros((size - after, step), jnp.float32)
            inverse_ref[after:, :] = inverse_ref[after:, :] - jnp.dot(
                lower, panel, precision=HIGHEST, preferred_element_type=jnp.float32
            )
    row = lax.broadcasted_iota(jnp.int32, (size, size), 0)
    col = lax.broadcasted_iota(jnp.int32, (size, size), 1)
    inverse_ref[...] = jnp.where(row >= col, inverse_ref[...], 0.0)


def inverse_factor(gram):
    size = gram.shape[0]
    return pl.pallas_call(
        functools.partial(factor_kernel, size=size),
        out_shape=jax.ShapeDtypeStruct((size, size), jnp.float32),
        in_specs=[pl.BlockSpec(memory_space=pltpu.VMEM)],
        out_specs=pl.BlockSpec(memory_space=pltpu.VMEM),
        compiler_params=pltpu.CompilerParams(vmem_limit_bytes=32 << 20),
        cost_estimate=pl.CostEstimate(flops=10**9, bytes_accessed=1 << 19, transcendentals=512),
        name="inverse_factor",
    )(gram)


def exchange(blocks, groups):
    return lax.all_to_all(blocks, AXES, 0, 0, axis_index_groups=groups, tiled=True)


def spread(block, groups):
    return exchange(jnp.broadcast_to(block[None], (len(groups[0]),) + block.shape), groups)


def spread_rows(block):
    return spread(spread(block, STRIDED), NEAR)


def add_up(blocks):
    parts = [blocks[i].astype(jnp.float32) for i in range(blocks.shape[0])]
    while len(parts) > 1:
        parts = [a + b for a, b in zip(parts[::2], parts[1::2])]
    return parts[0]


def total(block, groups):
    return add_up(spread(block, groups))


def to_tiles(blocks):
    rest = blocks.shape[1:]
    split = blocks.reshape((SIDE // 2, 2, SIDE // 2, 2, -1) + rest)
    return jnp.transpose(split, (1, 3, 0, 2, 4) + tuple(range(5, split.ndim))).reshape(blocks.shape)


def from_tiles(blocks):
    rest = blocks.shape[2:]
    split = blocks.reshape((2, 2, SIDE // 2, SIDE // 2, -1) + rest)
    order = (2, 0, 3, 1, 4) + tuple(range(5, split.ndim))
    return jnp.transpose(split, order).reshape((-1,) + rest)


def nt_dot(a, b, precision=None):
    return lax.dot_general(
        a, b, (((1,), (1,)), ((), ())), precision=precision, preferred_element_type=jnp.float32
    )


def body(momentum, gradient, right_factor):
    rows, cols = momentum.shape
    share_rank = right_factor.shape[0]
    groups, columns = SIDE * SIDE, LINE * CORES
    tiles = groups // 4
    rank = share_rank * groups
    blended = (momentum.astype(jnp.float32) + gradient.astype(jnp.float32)).astype(jnp.bfloat16)
    with jax.named_scope("factor_gather"):
        whole_factor = from_tiles(
            spread_rows(right_factor).reshape(4, tiles * share_rank, cols)
        )
    with jax.named_scope("basis"):
        basis = total(total(nt_dot(blended, whole_factor), CHIP), ROW)
    with jax.named_scope("gram"):
        share = rank // columns
        part = lax.dynamic_slice_in_dim(basis.T, lax.axis_index("tp") * share, share, 0)
        part = jnp.dot(part, basis, precision=HIGHEST)
        part = total(total(total(part, FAR), MIDDLE), NEAR)
        gram = spread(part, COLUMNS).reshape(rank, rank)
    with jax.named_scope("solve"):
        inverse = to_tiles(inverse_factor(gram))
        ortho_basis = nt_dot(basis, inverse, HIGHEST).astype(jnp.bfloat16)
    with jax.named_scope("projection"):
        partial = lax.dot_general(
            ortho_basis, blended, (((0,), (0,)), ((), ())), preferred_element_type=jnp.float32
        ).astype(jnp.bfloat16)
        partial = exchange(partial.reshape(4, tiles * share_rank, cols), NEAR)
        partial = add_up(partial).astype(jnp.bfloat16)
        partial = exchange(partial.reshape(tiles, share_rank, cols), STRIDED)
        own = add_up(partial)
        projection = spread_rows(own.astype(jnp.bfloat16)).reshape(rank, cols)
    with jax.named_scope("norms"):
        wide = projection.astype(jnp.float32)
        squares = total(jnp.sum(wide * wide, axis=1)[None], COLUMNS)[0]
        norms = jnp.sqrt(squares) + EPSILON
    with jax.named_scope("outputs"):
        carried = jnp.dot(ortho_basis, projection, preferred_element_type=jnp.float32)
        momentum_next = (blended.astype(jnp.float32) - (1.0 - MOMENTUM_DECAY) * carried).astype(
            jnp.bfloat16
        )
        scale_factor = math.sqrt(rows * groups * cols * columns / rank)
        factor = (wide / norms[:, None]).astype(jnp.bfloat16)
        direction = jnp.dot(ortho_basis, factor, preferred_element_type=jnp.float32)
        update = (scale_factor * direction).astype(jnp.bfloat16)
        z, y = lax.axis_index("fsdp") // SIDE, lax.axis_index("fsdp") % SIDE
        place = ((z % 2 * 2 + y % 2) * tiles + z // 2 * (SIDE // 2) + y // 2) * share_rank
        own_norms = lax.dynamic_slice_in_dim(norms, place, share_rank, 0)
        factor_next = own / own_norms[:, None]
    return (momentum_next, factor_next, update)


def solution(mesh):
    placed = P(*AXES)
    return jax.shard_map(
        body,
        mesh=mesh,
        in_specs=(placed, placed, placed),
        out_specs=(placed, placed, placed),
        check_vma=False,
    )
```

```python
import functools
import math

import jax
import jax.numpy as jnp
from jax import lax
from jax.experimental import pallas as pl
from jax.experimental.pallas import tpu as pltpu
from jax.sharding import PartitionSpec as P

EPSILON = 1e-06
MOMENTUM_DECAY = 0.95
HIGHEST = lax.Precision.HIGHEST

AXES = ("fsdp", "tp")
SIDE = 8
LINE = 4
CORES = 2


def groups_of(key, order):
    found = {}
    for index in range(SIDE * SIDE * LINE * CORES):
        fsdp, tp = divmod(index, LINE * CORES)
        place = divmod(fsdp, SIDE) + divmod(tp, CORES)
        found.setdefault(key(*place), []).append((order(*place), index))
    return [[index for _, index in sorted(group)] for group in found.values()]


def tile(place, core):
    return (place - core) % SIDE // 2


NEAR = groups_of(
    lambda z, y, x, core: (tile(z, core), tile(y, core), x, core), lambda z, y, x, core: (z % 2, y % 2)
)
STRIDED = groups_of(
    lambda z, y, x, core: (z % 2, y % 2, x, core), lambda z, y, x, core: (z // 2, y // 2)
)
FIRST_LINE = groups_of(
    lambda z, y, x, core: (z if core else y, x, core), lambda z, y, x, core: y if core else z
)
SECOND_LINE = groups_of(
    lambda z, y, x, core: (y if core else z, x, core), lambda z, y, x, core: z if core else y
)
CHIP = groups_of(lambda z, y, x, core: (z, y, x), lambda z, y, x, core: core)
ROW = groups_of(lambda z, y, x, core: (z, y, core), lambda z, y, x, core: x)
COLUMNS = groups_of(lambda z, y, x, core: (z, y), lambda z, y, x, core: (x, core))

FACTOR_BLOCK = 64
FACTOR_GROUP = 8


def block_inverse(block, size):
    lane = lax.broadcasted_iota(jnp.int32, (size, 128), 1)
    sub = lax.broadcasted_iota(jnp.int32, (size, 128), 0)
    eye = (lane == sub + size).astype(jnp.float32)
    if 2 * size == 128:
        work = jnp.concatenate([block, jnp.zeros_like(block)], axis=1) + eye
    else:
        work = jnp.concatenate([block, jnp.zeros((size, 128 - size), jnp.float32)], axis=1) + eye
    pivots = jnp.ones((size, 128), jnp.float32)
    for start in range(0, size, FACTOR_GROUP):
        columns = [
            jnp.broadcast_to(work[:, j : j + 1], (size, 128))
            for j in range(start, start + FACTOR_GROUP)
        ]
        for c in range(FACTOR_GROUP):
            j = start + c
            pivot = jnp.broadcast_to(columns[c][j : j + 1, :], (size, 128))
            ratio = jnp.where(sub > j, columns[c] * (1.0 / pivot), 0.0)
            pivots = jnp.where(sub == j, pivot, pivots)
            work = work - ratio * jnp.broadcast_to(work[j : j + 1, :], (size, 128))
            for later in range(c + 1, FACTOR_GROUP):
                columns[later] = columns[later] - ratio * jnp.broadcast_to(
                    columns[later][j : j + 1, :], (size, 128)
                )
    work = work * lax.rsqrt(pivots)
    return work[:, size : 2 * size]


def factor_kernel(gram_ref, inverse_ref, *, size):
    inverse_ref[...] = gram_ref[...]
    step = FACTOR_BLOCK
    for k in range(0, size, step):
        after = k + step
        inverse = block_inverse(inverse_ref[k:after, k:after], step)
        panel = jnp.dot(
            inverse, inverse_ref[k:after, :], precision=HIGHEST, preferred_element_type=jnp.float32
        )
        pieces = [inverse]
        if k > 0:
            pieces = [panel[:, :k]] + pieces
        if after < size:
            pieces = pieces + [panel[:, after:]]
            lower = lax.dot_general(
                inverse_ref[after:, k:after],
                inverse,
                (((1,), (1,)), ((), ())),
                precision=HIGHEST,
                preferred_element_type=jnp.float32,
            )
        panel = jnp.concatenate(pieces, axis=1)
        inverse_ref[k:after, :] = panel
        if after < size:
            inverse_ref[after:, k:after] = jnp.zeros((size - after, step), jnp.float32)
            inverse_ref[after:, :] = inverse_ref[after:, :] - jnp.dot(
                lower, panel, precision=HIGHEST, preferred_element_type=jnp.float32
            )
    row = lax.broadcasted_iota(jnp.int32, (size, size), 0)
    col = lax.broadcasted_iota(jnp.int32, (size, size), 1)
    inverse_ref[...] = jnp.where(row >= col, inverse_ref[...], 0.0)


def inverse_factor(gram):
    size = gram.shape[0]
    return pl.pallas_call(
        functools.partial(factor_kernel, size=size),
        out_shape=jax.ShapeDtypeStruct((size, size), jnp.float32),
        in_specs=[pl.BlockSpec(memory_space=pltpu.VMEM)],
        out_specs=pl.BlockSpec(memory_space=pltpu.VMEM),
        compiler_params=pltpu.CompilerParams(vmem_limit_bytes=32 << 20),
        cost_estimate=pl.CostEstimate(flops=10**9, bytes_accessed=1 << 19, transcendentals=512),
        name="inverse_factor",
    )(gram)


def exchange(blocks, groups):
    return lax.all_to_all(blocks, AXES, 0, 0, axis_index_groups=groups, tiled=True)


def spread(block, groups):
    return exchange(jnp.broadcast_to(block[None], (len(groups[0]),) + block.shape), groups)


def spread_rows(block):
    return spread(spread(block, STRIDED), NEAR)


def add_up(blocks):
    parts = [blocks[i].astype(jnp.float32) for i in range(blocks.shape[0])]
    while len(parts) > 1:
        parts = [a + b for a, b in zip(parts[::2], parts[1::2])]
    return parts[0]


def total(block, groups):
    return add_up(spread(block, groups))


def to_tiles(blocks):
    rest = blocks.shape[1:]
    split = blocks.reshape((SIDE // 2, 2, SIDE // 2, 2, -1) + rest)
    return jnp.transpose(split, (1, 3, 0, 2, 4) + tuple(range(5, split.ndim))).reshape(blocks.shape)


def nt_dot(a, b, precision=None):
    return lax.dot_general(
        a, b, (((1,), (1,)), ((), ())), precision=precision, preferred_element_type=jnp.float32
    )


def halves(block):
    middle = block.shape[1] // 2
    return jnp.concatenate([block[:, :middle], block[:, middle:]], axis=0)


def split_row(row, share):
    return row // (2 * share), row // share % 2, row % share


def exact_dot(a, selection):
    high = a.astype(jnp.bfloat16)
    rest = a - high.astype(jnp.float32)
    middle = rest.astype(jnp.bfloat16)
    low = (rest - middle.astype(jnp.float32)).astype(jnp.bfloat16)
    dot = functools.partial(jnp.dot, preferred_element_type=jnp.float32)
    return dot(high, selection) + (dot(middle, selection) + dot(low, selection))


def basis_kernel(momentum_ref, gradient_ref, factor_ref, blended_ref, copies_ref, *, share):
    blended = (
        momentum_ref[...].astype(jnp.float32) + gradient_ref[...].astype(jnp.float32)
    ).astype(jnp.bfloat16)
    blended_ref[...] = blended
    height, half = factor_ref.shape
    rank = height // 2
    place, part, low = split_row(lax.broadcasted_iota(jnp.int32, (height, rank), 0), share)
    parity, tile_index = place // 16, place % 16
    z = tile_index // 4 * 2 + parity // 2
    y = tile_index % 4 * 2 + parity % 2
    chosen = (z * SIDE + y) * share + low == lax.broadcasted_iota(jnp.int32, (height, rank), 1)
    result = None
    for h in range(2):
        product = nt_dot(blended[:, h * half : (h + 1) * half], factor_ref[...])
        selection = (chosen & (part == h)).astype(jnp.bfloat16)
        picked = exact_dot(product, selection)
        result = picked if result is None else result + picked
    for copy in range(copies_ref.shape[0]):
        copies_ref[copy] = result


def basis_part(momentum, gradient, factor, share):
    rows, cols = momentum.shape
    vmem = pl.BlockSpec(memory_space=pltpu.VMEM)
    return pl.pallas_call(
        functools.partial(basis_kernel, share=share),
        out_shape=(
            jax.ShapeDtypeStruct((rows, cols), jnp.bfloat16),
            jax.ShapeDtypeStruct((CORES, rows, factor.shape[0] // 2), jnp.float32),
        ),
        in_specs=[vmem] * 3,
        out_specs=(vmem, vmem),
        compiler_params=pltpu.CompilerParams(vmem_limit_bytes=32 << 20),
        name="basis_part",
    )(momentum, gradient, factor)


def half_columns(ortho, height, share, h):
    rank = ortho.shape[1]
    place, part, low = split_row(lax.broadcasted_iota(jnp.int32, (rank, height), 1), share)
    source = lax.broadcasted_iota(jnp.int32, (rank, height), 0)
    selection = ((place * share + low == source) & (part == h)).astype(jnp.bfloat16)
    return jnp.dot(ortho, selection, preferred_element_type=jnp.float32).astype(jnp.bfloat16)


def momentum_kernel(ortho_ref, projection_ref, blended_ref, out_ref, *, share):
    height, half = projection_ref.shape
    for h in range(2):
        columns = slice(h * half, (h + 1) * half)
        left = half_columns(ortho_ref[...], height, share, h)
        carried = jnp.dot(left, projection_ref[...], preferred_element_type=jnp.float32)
        out_ref[:, columns] = (
            blended_ref[:, columns].astype(jnp.float32) - (1.0 - MOMENTUM_DECAY) * carried
        ).astype(jnp.bfloat16)


def update_kernel(ortho_ref, projection_ref, squares_ref, out_ref, *, share, scale):
    height, half = projection_ref.shape
    rank = height // 2
    squares = jnp.broadcast_to(jnp.sum(squares_ref[...], axis=0), (8, height))
    place, _, low = split_row(lax.broadcasted_iota(jnp.int32, (height, rank), 0), share)
    target = lax.broadcasted_iota(jnp.int32, (height, rank), 1)
    fold = (place * share + low == target).astype(jnp.float32)
    norms = jnp.sqrt(jnp.dot(squares, fold, precision=HIGHEST, preferred_element_type=jnp.float32))
    inverse = 1.0 / (norms[0:1] + EPSILON)
    scaled = (ortho_ref[...].astype(jnp.float32) * inverse).astype(jnp.bfloat16)
    for h in range(2):
        left = half_columns(scaled, height, share, h)
        direction = jnp.dot(left, projection_ref[...], preferred_element_type=jnp.float32)
        out_ref[:, h * half : (h + 1) * half] = (scale * direction).astype(jnp.bfloat16)


def output_call(kernel, name, ortho, projection, extra):
    rows, cols = ortho.shape[0], 2 * projection.shape[1]
    vmem = pl.BlockSpec(memory_space=pltpu.VMEM)
    return pl.pallas_call(
        kernel,
        out_shape=jax.ShapeDtypeStruct((rows, cols), jnp.bfloat16),
        in_specs=[vmem] * 3,
        out_specs=vmem,
        compiler_params=pltpu.CompilerParams(vmem_limit_bytes=32 << 20),
        cost_estimate=pl.CostEstimate(
            flops=8 * rows * cols * ortho.shape[1], bytes_accessed=4 * rows * cols, transcendentals=0
        ),
        name=name,
    )(ortho, projection, extra)


def body(momentum, gradient, right_factor):
    rows, cols = momentum.shape
    share = right_factor.shape[0]
    groups, columns = SIDE * SIDE, LINE * CORES
    tiles = groups // 4
    rank = share * groups
    with jax.named_scope("factor_gather"):
        whole_factor = spread_rows(halves(right_factor)).reshape(2 * rank, cols // 2)
    with jax.named_scope("basis"):
        blended, copies = basis_part(momentum, gradient, whole_factor, share)
        basis = total(add_up(exchange(copies, CHIP)), ROW)
    with jax.named_scope("gram"):
        width = rank // columns
        part = lax.dynamic_slice_in_dim(basis.T, lax.axis_index("tp") * width, width, 0)
        part = jnp.dot(part, basis, precision=HIGHEST)
        part = total(total(part, FIRST_LINE), SECOND_LINE)
        gram = spread(part, COLUMNS).reshape(rank, rank)
    with jax.named_scope("solve"):
        inverse = to_tiles(inverse_factor(gram))
        ortho_basis = nt_dot(basis, inverse, HIGHEST).astype(jnp.bfloat16)
    with jax.named_scope("projection"):
        partial = lax.dot_general(
            ortho_basis, blended, (((0,), (0,)), ((), ())), preferred_element_type=jnp.float32
        ).astype(jnp.bfloat16)
        partial = exchange(partial.reshape(4, tiles * share, cols), NEAR)
        partial = add_up(partial).astype(jnp.bfloat16)
        partial = exchange(partial.reshape(tiles, share, cols), STRIDED)
        own = add_up(partial)
        projection = spread_rows(halves(own.astype(jnp.bfloat16))).reshape(2 * rank, cols // 2)
    with jax.named_scope("norms"):
        wide = projection.astype(jnp.float32)
        squares = spread(jnp.sum(wide * wide, axis=1)[None], COLUMNS)
    with jax.named_scope("outputs"):
        momentum_next = output_call(
            functools.partial(momentum_kernel, share=share),
            "momentum_next", ortho_basis, projection, blended,
        )
        scale = math.sqrt(rows * groups * cols * columns / rank)
        update = output_call(
            functools.partial(update_kernel, share=share, scale=scale),
            "update", ortho_basis, projection, squares,
        )
        z, y = lax.div(lax.axis_index("fsdp"), SIDE), lax.rem(lax.axis_index("fsdp"), SIDE)
        place = (lax.rem(z, 2) * 2 + lax.rem(y, 2)) * tiles + lax.div(z, 2) * (SIDE // 2) + lax.div(y, 2)
        own_squares = lax.dynamic_slice(
            squares, (0, 0, place * 2 * share), (columns, 1, 2 * share)
        )
        own_squares = jnp.sum(own_squares.reshape(2 * columns, share), axis=0)
        factor_next = own / (jnp.sqrt(own_squares) + EPSILON)[:, None]
    return (momentum_next, factor_next, update)


def solution(mesh):
    placed = P(*AXES)
    return jax.shard_map(
        body,
        mesh=mesh,
        in_specs=(placed, placed, placed),
        out_specs=(placed, placed, placed),
        check_vma=False,
    )
```

```python
import functools
import math

import jax
import jax.numpy as jnp
from jax import lax
from jax.experimental import pallas as pl
from jax.experimental.pallas import tpu as pltpu
from jax.sharding import PartitionSpec as P

EPSILON = 1e-06
MOMENTUM_DECAY = 0.95
HIGHEST = lax.Precision.HIGHEST

AXES = ("fsdp", "tp")
SIDE = 8
LINE = 4
CORES = 2


def groups_of(key, order):
    found = {}
    for index in range(SIDE * SIDE * LINE * CORES):
        fsdp, tp = divmod(index, LINE * CORES)
        place = divmod(fsdp, SIDE) + divmod(tp, CORES)
        found.setdefault(key(*place), []).append((order(*place), index))
    return [[index for _, index in sorted(group)] for group in found.values()]


def tile(place, core):
    return (place - core) % SIDE // 2


NEAR = groups_of(
    lambda z, y, x, core: (tile(z, core), tile(y, core), x, core), lambda z, y, x, core: (z % 2, y % 2)
)
STRIDED = groups_of(
    lambda z, y, x, core: (z % 2, y % 2, x, core), lambda z, y, x, core: (z // 2, y // 2)
)
PLANE = groups_of(lambda z, y, x, core: (x, core), lambda z, y, x, core: (z, y))
CHIP = groups_of(lambda z, y, x, core: (z, y, x), lambda z, y, x, core: core)
ROW = groups_of(lambda z, y, x, core: (z, y, core), lambda z, y, x, core: x)
COLUMNS = groups_of(lambda z, y, x, core: (z, y), lambda z, y, x, core: (x, core))

FACTOR_BLOCK = 64
FACTOR_GROUP = 16


def block_inverse(block, size):
    lane = lax.broadcasted_iota(jnp.int32, (size, 128), 1)
    sub = lax.broadcasted_iota(jnp.int32, (size, 128), 0)
    eye = (lane == sub + size).astype(jnp.float32)
    if 2 * size == 128:
        work = jnp.concatenate([block, jnp.zeros_like(block)], axis=1) + eye
    else:
        work = jnp.concatenate([block, jnp.zeros((size, 128 - size), jnp.float32)], axis=1) + eye
    pivots = jnp.ones((size, 128), jnp.float32)
    for start in range(0, size, FACTOR_GROUP):
        columns = [
            jnp.broadcast_to(work[:, j : j + 1], (size, 128))
            for j in range(start, start + FACTOR_GROUP)
        ]
        for c in range(FACTOR_GROUP):
            j = start + c
            pivot = jnp.broadcast_to(columns[c][j : j + 1, :], (size, 128))
            ratio = jnp.where(sub > j, columns[c] * (1.0 / pivot), 0.0)
            pivots = jnp.where(sub == j, pivot, pivots)
            work = work - ratio * jnp.broadcast_to(work[j : j + 1, :], (size, 128))
            for later in range(c + 1, FACTOR_GROUP):
                columns[later] = columns[later] - ratio * jnp.broadcast_to(
                    columns[later][j : j + 1, :], (size, 128)
                )
    work = work * lax.rsqrt(pivots)
    return work[:, size : 2 * size]


def factor_in_place(inverse_ref):
    size = inverse_ref.shape[0]
    step = FACTOR_BLOCK
    for k in range(0, size, step):
        after = k + step
        inverse = block_inverse(inverse_ref[k:after, k:after], step)
        panel = jnp.dot(
            inverse, inverse_ref[k:after, :], precision=HIGHEST, preferred_element_type=jnp.float32
        )
        pieces = [inverse]
        if k > 0:
            pieces = [panel[:, :k]] + pieces
        if after < size:
            pieces = pieces + [panel[:, after:]]
            lower = nt_dot(inverse_ref[after:, k:after], inverse, HIGHEST)
        panel = jnp.concatenate(pieces, axis=1)
        inverse_ref[k:after, :] = panel
        if after < size:
            inverse_ref[after:, k:after] = jnp.zeros((size - after, step), jnp.float32)
            inverse_ref[after:, :] = inverse_ref[after:, :] - jnp.dot(
                lower, panel, precision=HIGHEST, preferred_element_type=jnp.float32
            )


def gram_kernel(parts_ref, basis_ref, blocks_ref):
    basis = (parts_ref[0] + parts_ref[1]) + (parts_ref[2] + parts_ref[3])
    basis_ref[...] = basis
    gram = jnp.dot(basis.T, basis, precision=HIGHEST, preferred_element_type=jnp.float32)
    halves_of_row = gram.shape[1] // 128
    for block in range(blocks_ref.shape[0]):
        row, col = 8 * (block // halves_of_row), 128 * (block % halves_of_row)
        blocks_ref[block] = gram[row : row + 8, col : col + 128]


def copies_kernel(parts_ref, copies_ref):
    copies_ref[...] = jnp.broadcast_to(jnp.sum(parts_ref[...], axis=0)[None], copies_ref.shape)


def solve_kernel(blocks_ref, basis_ref, ortho_ref, inverse_ref, *, share):
    size = inverse_ref.shape[0]
    for block in range(blocks_ref.shape[0]):
        row, col = 8 * (block // (size // 128)), 128 * (block % (size // 128))
        inverse_ref[row : row + 8, col : col + 128] = blocks_ref[block]
    factor_in_place(inverse_ref)
    source = lax.broadcasted_iota(jnp.int32, (size, size), 0)
    target = lax.broadcasted_iota(jnp.int32, (size, size), 1)
    inverse = jnp.where(source >= target, inverse_ref[...], 0.0)
    ortho = nt_dot(basis_ref[...], inverse, HIGHEST).astype(jnp.bfloat16)
    selection = (device_of(target // share) * share + target % share == source).astype(jnp.bfloat16)
    ortho_ref[...] = jnp.dot(ortho, selection, preferred_element_type=jnp.float32).astype(
        jnp.bfloat16
    )


VMEM = pl.BlockSpec(memory_space=pltpu.VMEM)


def local_call(kernel, name, shapes, *operands, scratch=(), flops=0):
    size = sum(math.prod(o.shape) * o.dtype.itemsize for o in operands)
    return pl.pallas_call(
        kernel,
        out_shape=shapes,
        in_specs=[VMEM] * len(operands),
        out_specs=jax.tree.map(lambda _: VMEM, shapes),
        scratch_shapes=scratch,
        compiler_params=pltpu.CompilerParams(vmem_limit_bytes=32 << 20),
        cost_estimate=pl.CostEstimate(flops=flops, bytes_accessed=2 * size, transcendentals=0),
        name=name,
    )(*operands)


def shaped(*shape, dtype=jnp.float32):
    return jax.ShapeDtypeStruct(shape, dtype)


def exchange(blocks, groups):
    return lax.all_to_all(blocks, AXES, 0, 0, axis_index_groups=groups, tiled=True)


def spread(block, groups):
    return exchange(jnp.broadcast_to(block[None], (len(groups[0]),) + block.shape), groups)


def spread_rows(block):
    return spread(spread(block, STRIDED), NEAR)


def add_up(blocks):
    parts = [blocks[i].astype(jnp.float32) for i in range(blocks.shape[0])]
    while len(parts) > 1:
        parts = [a + b for a, b in zip(parts[::2], parts[1::2])]
    return parts[0]


def total(block, groups):
    return add_up(spread(block, groups))


def device_of(place):
    parity, tile_index = place // 16, place % 16
    z = tile_index // 4 * 2 + parity // 2
    y = tile_index % 4 * 2 + parity % 2
    return z * SIDE + y


def nt_dot(a, b, precision=None):
    return lax.dot_general(
        a, b, (((1,), (1,)), ((), ())), precision=precision, preferred_element_type=jnp.float32
    )


def halves(block):
    middle = block.shape[1] // 2
    return jnp.concatenate([block[:, :middle], block[:, middle:]], axis=0)


def split_row(row, share):
    return row // (2 * share), row // share % 2, row % share


def exact_dot(a, selection):
    high = a.astype(jnp.bfloat16)
    rest = a - high.astype(jnp.float32)
    middle = rest.astype(jnp.bfloat16)
    low = (rest - middle.astype(jnp.float32)).astype(jnp.bfloat16)
    dot = functools.partial(jnp.dot, preferred_element_type=jnp.float32)
    return dot(high, selection) + (dot(middle, selection) + dot(low, selection))


def basis_kernel(momentum_ref, gradient_ref, factor_ref, blended_ref, copies_ref, *, share):
    blended = (
        momentum_ref[...].astype(jnp.float32) + gradient_ref[...].astype(jnp.float32)
    ).astype(jnp.bfloat16)
    blended_ref[...] = blended
    height, half = factor_ref.shape
    rank = height // 2
    place, part, low = split_row(lax.broadcasted_iota(jnp.int32, (height, rank), 0), share)
    chosen = device_of(place) * share + low == lax.broadcasted_iota(jnp.int32, (height, rank), 1)
    result = None
    for h in range(2):
        product = nt_dot(blended[:, h * half : (h + 1) * half], factor_ref[...])
        selection = (chosen & (part == h)).astype(jnp.bfloat16)
        picked = exact_dot(product, selection)
        result = picked if result is None else result + picked
    for copy in range(copies_ref.shape[0]):
        copies_ref[copy] = result


def half_columns(ortho, height, share, h):
    rank = ortho.shape[1]
    place, part, low = split_row(lax.broadcasted_iota(jnp.int32, (rank, height), 1), share)
    source = lax.broadcasted_iota(jnp.int32, (rank, height), 0)
    selection = ((place * share + low == source) & (part == h)).astype(jnp.bfloat16)
    return jnp.dot(ortho, selection, preferred_element_type=jnp.float32).astype(jnp.bfloat16)


def momentum_kernel(ortho_ref, projection_ref, blended_ref, out_ref, *, share):
    height, half = projection_ref.shape
    for h in range(2):
        columns = slice(h * half, (h + 1) * half)
        left = half_columns(ortho_ref[...], height, share, h)
        carried = jnp.dot(left, projection_ref[...], preferred_element_type=jnp.float32)
        out_ref[:, columns] = (
            blended_ref[:, columns].astype(jnp.float32) - (1.0 - MOMENTUM_DECAY) * carried
        ).astype(jnp.bfloat16)


def squares_kernel(projection_ref, copies_ref):
    height, half = projection_ref.shape
    wide = projection_ref[...].astype(jnp.float32)
    squares = wide * wide
    high = squares.astype(jnp.bfloat16)
    low = (squares - high.astype(jnp.float32)).astype(jnp.bfloat16)
    ones = jnp.ones((8, half), jnp.bfloat16)
    sums = nt_dot(ones, high) + nt_dot(ones, low)
    copies_ref[...] = jnp.zeros(copies_ref.shape, jnp.float32)
    for copy in range(copies_ref.shape[0]):
        for piece in range(height // 128):
            copies_ref[copy, piece : piece + 1, :] = sums[0:1, piece * 128 : (piece + 1) * 128]


def update_kernel(
    ortho_ref, projection_ref, squares_ref, own_ref, out_ref, factor_ref, *, share, scale
):
    height, half = projection_ref.shape
    rank = height // 2
    pieces = jnp.sum(squares_ref[...], axis=0)
    squares = jnp.concatenate([pieces[i : i + 1] for i in range(height // 128)], axis=1)
    place, _, low = split_row(lax.broadcasted_iota(jnp.int32, (height, rank), 0), share)
    target = lax.broadcasted_iota(jnp.int32, (height, rank), 1)
    fold = (place * share + low == target).astype(jnp.float32)
    squares = jnp.dot(
        jnp.broadcast_to(squares, (8, height)),
        fold,
        precision=HIGHEST,
        preferred_element_type=jnp.float32,
    )
    inverse = 1.0 / (jnp.sqrt(squares) + EPSILON)
    scaled = (ortho_ref[...].astype(jnp.float32) * inverse[0:1]).astype(jnp.bfloat16)
    for h in range(2):
        left = half_columns(scaled, height, share, h)
        direction = jnp.dot(left, projection_ref[...], preferred_element_type=jnp.float32)
        out_ref[:, h * half : (h + 1) * half] = (scale * direction).astype(jnp.bfloat16)
    column = lax.broadcasted_iota(jnp.int32, (8, rank), 1)
    natural = device_of(column // share) * share + column % share
    first = lax.axis_index("fsdp") * share
    mine = natural == first + lax.broadcasted_iota(jnp.int32, (8, rank), 0)
    own_inverse = jnp.sum(jnp.where(mine, inverse, 0.0), axis=1, keepdims=True)
    factor_ref[...] = own_ref[...] * own_inverse[0:share]


def body(momentum, gradient, right_factor):
    rows, cols = momentum.shape
    share = right_factor.shape[0]
    groups, columns = SIDE * SIDE, LINE * CORES
    tiles = groups // 4
    rank = share * groups
    with jax.named_scope("factor_gather"):
        whole_factor = spread_rows(halves(right_factor)).reshape(2 * rank, cols // 2)
    with jax.named_scope("basis"):
        blended, copies = local_call(
            functools.partial(basis_kernel, share=share),
            "basis_part",
            (shaped(rows, cols, dtype=jnp.bfloat16), shaped(CORES, rows, rank)),
            momentum, gradient, whole_factor,
        )
        parts = spread(add_up(exchange(copies, CHIP)), ROW)
    with jax.named_scope("gram"):
        basis, blocks = local_call(
            gram_kernel,
            "gram_part",
            (shaped(rows, rank), shaped(groups, 8, rank * rank // groups // 8)),
            parts,
        )
        parts = exchange(blocks, PLANE)
        copies = local_call(copies_kernel, "gram_copies", shaped(*parts.shape), parts)
        blocks = exchange(copies, PLANE)
    with jax.named_scope("solve"):
        ortho_basis = local_call(
            functools.partial(solve_kernel, share=share),
            "ortho_basis",
            shaped(rows, rank, dtype=jnp.bfloat16),
            blocks, basis,
            scratch=[pltpu.VMEM((rank, rank), jnp.float32)],
            flops=10**9,
        )
    with jax.named_scope("projection"):
        partial = lax.dot_general(
            ortho_basis, blended, (((0,), (0,)), ((), ())), preferred_element_type=jnp.float32
        ).astype(jnp.bfloat16)
        partial = exchange(partial.reshape(4, tiles * share, cols), NEAR)
        partial = add_up(partial).astype(jnp.bfloat16)
        partial = exchange(partial.reshape(tiles, share, cols), STRIDED)
        own = add_up(partial)
        projection = spread_rows(halves(own.astype(jnp.bfloat16))).reshape(2 * rank, cols // 2)
    with jax.named_scope("norms"):
        copies = local_call(squares_kernel, "squares", shaped(columns, 8, 128), projection)
        squares = exchange(copies, COLUMNS)
    with jax.named_scope("outputs"):
        momentum_next = local_call(
            functools.partial(momentum_kernel, share=share),
            "momentum_next",
            shaped(rows, cols, dtype=jnp.bfloat16),
            ortho_basis, projection, blended,
            flops=8 * rows * cols * rank,
        )
        scale = math.sqrt(rows * groups * cols * columns / rank)
        update, factor_next = local_call(
            functools.partial(update_kernel, share=share, scale=scale),
            "update",
            (shaped(rows, cols, dtype=jnp.bfloat16), shaped(share, cols)),
            ortho_basis, projection, squares, own,
            flops=8 * rows * cols * rank,
        )
    return (momentum_next, factor_next, update)


def solution(mesh):
    placed = P(*AXES)
    return jax.shard_map(
        body,
        mesh=mesh,
        in_specs=(placed, placed, placed),
        out_specs=(placed, placed, placed),
        check_vma=False,
    )
```

```python
import functools
import math

import jax
import jax.numpy as jnp
from jax import lax
from jax.experimental import pallas as pl
from jax.experimental.pallas import tpu as pltpu
from jax.sharding import PartitionSpec as P

EPSILON = 1e-06
MOMENTUM_DECAY = 0.95
HIGHEST = lax.Precision.HIGHEST

AXES = ("fsdp", "tp")
SIDE = 8
LINE = 4
CORES = 2


def groups_of(key, order):
    found = {}
    for index in range(SIDE * SIDE * LINE * CORES):
        fsdp, tp = divmod(index, LINE * CORES)
        place = divmod(fsdp, SIDE) + divmod(tp, CORES)
        found.setdefault(key(*place), []).append((order(*place), index))
    return [[index for _, index in sorted(group)] for group in found.values()]


def tile(place, core):
    return (place - core) % SIDE // 2


NEAR = groups_of(
    lambda z, y, x, core: (tile(z, core), tile(y, core), x, core), lambda z, y, x, core: (z % 2, y % 2)
)
STRIDED = groups_of(
    lambda z, y, x, core: (z % 2, y % 2, x, core), lambda z, y, x, core: (z // 2, y // 2)
)
PLANE = groups_of(lambda z, y, x, core: (x, core), lambda z, y, x, core: (z, y))
ROW = groups_of(lambda z, y, x, core: (z, y, core), lambda z, y, x, core: x)
COLUMNS = groups_of(lambda z, y, x, core: (z, y), lambda z, y, x, core: (x, core))

FACTOR_BLOCK = 64
FACTOR_GROUP = 16


def block_inverse(block, size):
    sub = lax.broadcasted_iota(jnp.int32, (size, 128), 0)
    eye = (lax.broadcasted_iota(jnp.int32, (size, 128), 1) == sub + size).astype(jnp.float32)
    work = jnp.concatenate([block, jnp.zeros((size, 128 - size), jnp.float32)], axis=1) + eye
    pivots = jnp.ones((size, 128), jnp.float32)

    def row(array, index):
        return jnp.broadcast_to(array[index : index + 1, :], (size, 128))

    for start in range(0, size, FACTOR_GROUP):
        columns = [
            jnp.broadcast_to(work[:, j : j + 1], (size, 128))
            for j in range(start, start + FACTOR_GROUP)
        ]
        for c in range(0, FACTOR_GROUP, 2):
            j = start + c
            first, second = columns[c], columns[c + 1]
            a, e, b = row(first, j), row(first, j + 1), row(second, j + 1)
            det = a * b - e * e
            inverse_det, inverse_a = 1.0 / det, 1.0 / a
            ratio = jnp.where(sub > j + 1, (first * b - second * e) * inverse_det, 0.0)
            ratio = jnp.where(sub == j + 1, e * inverse_a, ratio)
            other = jnp.where(sub > j + 1, (second * a - first * e) * inverse_det, 0.0)
            pivots = jnp.where(sub == j, a, jnp.where(sub == j + 1, det * inverse_a, pivots))
            for later in range(c + 2, FACTOR_GROUP):
                column = columns[later]
                columns[later] = column - ratio * row(column, j) - other * row(column, j + 1)
            work = work - ratio * row(work, j) - other * row(work, j + 1)
    work = work * lax.rsqrt(pivots)
    return work[:, size : 2 * size]


def factor_in_place(inverse_ref):
    size = inverse_ref.shape[0]
    step = FACTOR_BLOCK
    for k in range(0, size, step):
        after = k + step
        inverse = block_inverse(inverse_ref[k:after, k:after], step)
        panel = jnp.dot(
            inverse, inverse_ref[k:after, :], precision=HIGHEST, preferred_element_type=jnp.float32
        )
        pieces = [inverse]
        if k > 0:
            pieces = [panel[:, :k]] + pieces
        if after < size:
            pieces = pieces + [panel[:, after:]]
            lower = nt_dot(inverse_ref[after:, k:after], inverse, HIGHEST)
        panel = jnp.concatenate(pieces, axis=1)
        inverse_ref[k:after, :] = panel
        if after < size:
            inverse_ref[after:, k:after] = jnp.zeros((size - after, step), jnp.float32)
            inverse_ref[after:, :] = inverse_ref[after:, :] - jnp.dot(
                lower, panel, precision=HIGHEST, preferred_element_type=jnp.float32
            )


def gram_kernel(parts_ref, basis_ref, blocks_ref):
    basis = (parts_ref[0] + parts_ref[1]) + (parts_ref[2] + parts_ref[3])
    basis_ref[...] = basis
    gram = jnp.dot(basis.T, basis, precision=HIGHEST, preferred_element_type=jnp.float32)
    halves_of_row = gram.shape[1] // 128
    for block in range(blocks_ref.shape[0]):
        row, col = 8 * (block // halves_of_row), 128 * (block % halves_of_row)
        blocks_ref[block] = gram[row : row + 8, col : col + 128]


def copies_kernel(parts_ref, copies_ref):
    copies_ref[...] = jnp.broadcast_to(jnp.sum(parts_ref[...], axis=0)[None], copies_ref.shape)


def solve_kernel(blocks_ref, basis_ref, ortho_ref, inverse_ref, *, share):
    size = inverse_ref.shape[0]
    for block in range(blocks_ref.shape[0]):
        row, col = 8 * (block // (size // 128)), 128 * (block % (size // 128))
        inverse_ref[row : row + 8, col : col + 128] = blocks_ref[block]
    source = lax.broadcasted_iota(jnp.int32, (size, size), 0)
    target = lax.broadcasted_iota(jnp.int32, (size, size), 1)
    diagonal = jnp.where(source == target, inverse_ref[...], 0.0)
    scale_row = lax.rsqrt(jnp.sum(diagonal, axis=0, keepdims=True))
    scale_column = lax.rsqrt(jnp.sum(diagonal, axis=1, keepdims=True))
    inverse_ref[...] = inverse_ref[...] * scale_column * scale_row
    factor_in_place(inverse_ref)
    inverse = jnp.where(source >= target, inverse_ref[...] * scale_row, 0.0)
    ortho = nt_dot(basis_ref[...], inverse, HIGHEST).astype(jnp.bfloat16)
    selection = (device_of(target // share) * share + target % share == source).astype(jnp.bfloat16)
    ortho_ref[...] = jnp.dot(ortho, selection, preferred_element_type=jnp.float32).astype(
        jnp.bfloat16
    )


VMEM = pl.BlockSpec(memory_space=pltpu.VMEM)


def local_call(kernel, name, shapes, *operands, scratch=(), flops=0):
    size = sum(math.prod(o.shape) * o.dtype.itemsize for o in operands)
    return pl.pallas_call(
        kernel,
        out_shape=shapes,
        in_specs=[VMEM] * len(operands),
        out_specs=jax.tree.map(lambda _: VMEM, shapes),
        scratch_shapes=scratch,
        compiler_params=pltpu.CompilerParams(vmem_limit_bytes=32 << 20),
        cost_estimate=pl.CostEstimate(flops=flops, bytes_accessed=2 * size, transcendentals=0),
        name=name,
    )(*operands)


def shaped(*shape, dtype=jnp.float32):
    return jax.ShapeDtypeStruct(shape, dtype)


def exchange(blocks, groups):
    return lax.all_to_all(blocks, AXES, 0, 0, axis_index_groups=groups, tiled=True)


def spread(block, groups):
    return exchange(jnp.broadcast_to(block[None], (len(groups[0]),) + block.shape), groups)


def spread_rows(block):
    return spread(spread(block, STRIDED), NEAR)


def add_up(blocks):
    parts = [blocks[i].astype(jnp.float32) for i in range(blocks.shape[0])]
    while len(parts) > 1:
        parts = [a + b for a, b in zip(parts[::2], parts[1::2])]
    return parts[0]


def device_of(place):
    parity, tile_index = place // 16, place % 16
    z = tile_index // 4 * 2 + parity // 2
    y = tile_index % 4 * 2 + parity % 2
    return z * SIDE + y


def nt_dot(a, b, precision=None):
    return lax.dot_general(
        a, b, (((1,), (1,)), ((), ())), precision=precision, preferred_element_type=jnp.float32
    )


def halves(block):
    middle = block.shape[1] // 2
    return jnp.concatenate([block[:, :middle], block[:, middle:]], axis=0)


def split_row(row, share):
    return row // (2 * share), row // share % 2, row % share


def exact_dot(a, selection):
    high = a.astype(jnp.bfloat16)
    rest = a - high.astype(jnp.float32)
    middle = rest.astype(jnp.bfloat16)
    low = (rest - middle.astype(jnp.float32)).astype(jnp.bfloat16)
    dot = functools.partial(jnp.dot, preferred_element_type=jnp.float32)
    return dot(high, selection) + (dot(middle, selection) + dot(low, selection))


def basis_kernel(momentum_ref, gradient_ref, factor_ref, blended_ref, basis_ref, *, share):
    blended = (
        momentum_ref[...].astype(jnp.float32) + gradient_ref[...].astype(jnp.float32)
    ).astype(jnp.bfloat16)
    blended_ref[...] = blended
    height, half = factor_ref.shape
    rank = height // 2
    place, _, low = split_row(lax.broadcasted_iota(jnp.int32, (height, rank), 0), share)
    target = lax.broadcasted_iota(jnp.int32, (height, rank), 1)
    selection = (device_of(place) * share + low == target).astype(jnp.bfloat16)
    _, part, _ = split_row(lax.broadcasted_iota(jnp.int32, (blended.shape[0], height), 1), share)
    left = nt_dot(blended[:, :half], factor_ref[...])
    right = nt_dot(blended[:, half:], factor_ref[...])
    basis_ref[...] = exact_dot(jnp.where(part == 0, left, right), selection)


def momentum_kernel(ortho_ref, projection_ref, blended_ref, out_ref, left_ref, *, share):
    height, half = projection_ref.shape
    rank = height // 2
    place, part, low = split_row(lax.broadcasted_iota(jnp.int32, (rank, height), 1), share)
    source = lax.broadcasted_iota(jnp.int32, (rank, height), 0)
    for h in range(2):
        columns = slice(h * half, (h + 1) * half)
        selection = ((place * share + low == source) & (part == h)).astype(jnp.bfloat16)
        left = jnp.dot(ortho_ref[...], selection, preferred_element_type=jnp.float32)
        left = left.astype(jnp.bfloat16)
        left_ref[h] = left
        carried = jnp.dot(left, projection_ref[...], preferred_element_type=jnp.float32)
        out_ref[:, columns] = (
            blended_ref[:, columns].astype(jnp.float32) - (1.0 - MOMENTUM_DECAY) * carried
        ).astype(jnp.bfloat16)


def squares_kernel(projection_ref, copies_ref):
    height, half = projection_ref.shape
    sums = jnp.zeros((height, 128), jnp.float32)
    for column in range(0, half, 128):
        piece = projection_ref[:, column : column + 128].astype(jnp.float32)
        sums = sums + piece * piece
    totals = nt_dot(jnp.ones((8, 128), jnp.float32), sums, HIGHEST)
    copies_ref[...] = jnp.zeros(copies_ref.shape, jnp.float32)
    for copy in range(copies_ref.shape[0]):
        for piece in range(height // 128):
            copies_ref[copy, piece : piece + 1, :] = totals[0:1, piece * 128 : (piece + 1) * 128]


def update_kernel(left_ref, projection_ref, squares_ref, own_ref, out_ref, factor_ref, *, share, scale):
    height, half = projection_ref.shape
    pieces = jnp.sum(squares_ref[...], axis=0)
    squares = jnp.concatenate([pieces[i : i + 1] for i in range(height // 128)], axis=1)
    squares = jnp.broadcast_to(squares, (8, height))
    place, part, low = split_row(lax.broadcasted_iota(jnp.int32, (8, height), 1), share)
    other = jnp.where(
        part == 0, pltpu.roll(squares, height - share, 1), pltpu.roll(squares, share, 1)
    )
    inverse = 1.0 / (jnp.sqrt(squares + other) + EPSILON)
    for h in range(2):
        left = (left_ref[h].astype(jnp.float32) * inverse[0:1]).astype(jnp.bfloat16)
        direction = jnp.dot(left, projection_ref[...], preferred_element_type=jnp.float32)
        out_ref[:, h * half : (h + 1) * half] = (scale * direction).astype(jnp.bfloat16)
    mine = (device_of(place) == lax.axis_index("fsdp")) & (part == 0)
    mine = mine & (low == lax.broadcasted_iota(jnp.int32, (8, height), 0))
    own_inverse = jnp.sum(jnp.where(mine, inverse, 0.0), axis=1, keepdims=True)
    factor_ref[...] = own_ref[...] * own_inverse[0:share]


def body(momentum, gradient, right_factor):
    rows, cols = momentum.shape
    share = right_factor.shape[0]
    groups, columns = SIDE * SIDE, LINE * CORES
    tiles = groups // 4
    rank = share * groups
    with jax.named_scope("factor_gather"):
        whole_factor = spread_rows(halves(right_factor)).reshape(2 * rank, cols // 2)
    with jax.named_scope("basis"):
        blended, part = local_call(
            functools.partial(basis_kernel, share=share),
            "basis_part",
            (shaped(rows, cols, dtype=jnp.bfloat16), shaped(rows, rank)),
            momentum, gradient, whole_factor,
        )
        other_core = [(i, i ^ 1) for i in range(columns)]
        parts = spread(part + lax.ppermute(part, "tp", other_core), ROW)
    with jax.named_scope("gram"):
        basis, blocks = local_call(
            gram_kernel,
            "gram_part",
            (shaped(rows, rank), shaped(groups, 8, rank * rank // groups // 8)),
            parts,
        )
        parts = exchange(blocks, PLANE)
        copies = local_call(copies_kernel, "gram_copies", shaped(*parts.shape), parts)
        blocks = exchange(copies, PLANE)
    with jax.named_scope("solve"):
        ortho_basis = local_call(
            functools.partial(solve_kernel, share=share),
            "ortho_basis",
            shaped(rows, rank, dtype=jnp.bfloat16),
            blocks, basis,
            scratch=[pltpu.VMEM((rank, rank), jnp.float32)],
            flops=10**9,
        )
    with jax.named_scope("projection"):
        partial = lax.dot_general(
            ortho_basis, blended, (((0,), (0,)), ((), ())), preferred_element_type=jnp.float32
        ).astype(jnp.bfloat16)
        partial = exchange(partial.reshape(4, tiles * share, cols), NEAR)
        partial = add_up(partial).astype(jnp.bfloat16)
        partial = exchange(partial.reshape(tiles, share, cols), STRIDED)
        own = add_up(partial)
        projection = spread_rows(halves(own.astype(jnp.bfloat16))).reshape(2 * rank, cols // 2)
    with jax.named_scope("norms"):
        copies = local_call(squares_kernel, "squares", shaped(columns, 8, 128), projection)
        squares = exchange(copies, COLUMNS)
    with jax.named_scope("outputs"):
        momentum_next, left = local_call(
            functools.partial(momentum_kernel, share=share),
            "momentum_next",
            (shaped(rows, cols, dtype=jnp.bfloat16), shaped(2, rows, 2 * rank, dtype=jnp.bfloat16)),
            ortho_basis, projection, blended,
            flops=8 * rows * cols * rank,
        )
        scale = math.sqrt(rows * groups * cols * columns / rank)
        update, factor_next = local_call(
            functools.partial(update_kernel, share=share, scale=scale),
            "update",
            (shaped(rows, cols, dtype=jnp.bfloat16), shaped(share, cols)),
            left, projection, squares, own,
            flops=8 * rows * cols * rank,
        )
    return (momentum_next, factor_next, update)


def solution(mesh):
    placed = P(*AXES)
    return jax.shard_map(
        body,
        mesh=mesh,
        in_specs=(placed, placed, placed),
        out_specs=(placed, placed, placed),
        check_vma=False,
    )
```

```python
import functools
import math

import jax
import jax.numpy as jnp
from jax import lax
from jax.experimental import pallas as pl
from jax.experimental.pallas import tpu as pltpu
from jax.sharding import PartitionSpec as P

EPSILON = 1e-06
MOMENTUM_DECAY = 0.95
HIGHEST = lax.Precision.HIGHEST

AXES = ("fsdp", "tp")
SIDE = 8
LINE = 4
CORES = 2


def groups_of(key, order):
    found = {}
    for index in range(SIDE * SIDE * LINE * CORES):
        fsdp, tp = divmod(index, LINE * CORES)
        place = divmod(fsdp, SIDE) + divmod(tp, CORES)
        found.setdefault(key(*place), []).append((order(*place), index))
    return [[index for _, index in sorted(group)] for group in found.values()]


def tile(place, core):
    return (place - core) % SIDE // 2


NEAR = groups_of(
    lambda z, y, x, core: (tile(z, core), tile(y, core), x, core), lambda z, y, x, core: (z % 2, y % 2)
)
STRIDED = groups_of(
    lambda z, y, x, core: (z % 2, y % 2, x, core), lambda z, y, x, core: (z // 2, y // 2)
)
PLANE = groups_of(lambda z, y, x, core: (x, core), lambda z, y, x, core: (z, y))
ROW = groups_of(lambda z, y, x, core: (z, y, core), lambda z, y, x, core: x)
COLUMNS = groups_of(lambda z, y, x, core: (z, y), lambda z, y, x, core: (x, core))

FACTOR_BLOCK = 64
FACTOR_GROUP = 16


def block_inverse(block, size):
    sub = lax.broadcasted_iota(jnp.int32, (size, 128), 0)
    eye = (lax.broadcasted_iota(jnp.int32, (size, 128), 1) == sub + size).astype(jnp.float32)
    work = jnp.concatenate([block, jnp.zeros((size, 128 - size), jnp.float32)], axis=1) + eye
    done = []
    for start in range(0, size, FACTOR_GROUP):
        height = size - start
        sub = lax.broadcasted_iota(jnp.int32, (height, 128), 0)

        def row(array, index):
            return jnp.broadcast_to(array[index : index + 1, :], (height, 128))

        pivots = jnp.ones((height, 128), jnp.float32)
        columns = [
            jnp.broadcast_to(work[:, start + j : start + j + 1], (height, 128))
            for j in range(FACTOR_GROUP)
        ]
        for j in range(0, FACTOR_GROUP, 2):
            first, second = columns[j], columns[j + 1]
            a, e, b = row(first, j), row(first, j + 1), row(second, j + 1)
            det = a * b - e * e
            inverse_det, inverse_a = 1.0 / det, 1.0 / a
            ratio = jnp.where(sub > j + 1, (first * b - second * e) * inverse_det, 0.0)
            ratio = jnp.where(sub == j + 1, e * inverse_a, ratio)
            other = jnp.where(sub > j + 1, (second * a - first * e) * inverse_det, 0.0)
            pivots = jnp.where(sub == j, a, jnp.where(sub == j + 1, det * inverse_a, pivots))
            for later in range(j + 2, FACTOR_GROUP):
                column = columns[later]
                columns[later] = column - ratio * row(column, j) - other * row(column, j + 1)
            work = work - ratio * row(work, j) - other * row(work, j + 1)
        done.append(work[:FACTOR_GROUP] * lax.rsqrt(pivots[:FACTOR_GROUP]))
        work = work[FACTOR_GROUP:]
    return jnp.concatenate(done, axis=0)[:, size : 2 * size]


def inverse_factor(rows):
    step = FACTOR_BLOCK
    rows = list(rows)
    count = len(rows)

    def with_column(row, k, block):
        pieces = [row[:, q * step : (q + 1) * step] for q in range(count)]
        return jnp.concatenate(pieces[:k] + [block] + pieces[k + 1 :], axis=1)

    for k in range(count):
        inverse = block_inverse(rows[k][:, k * step : (k + 1) * step], step)
        panel = jnp.dot(inverse, rows[k], precision=HIGHEST, preferred_element_type=jnp.float32)
        rows[k] = with_column(panel, k, inverse)
        for i in range(k + 1, count):
            lower = nt_dot(rows[i][:, k * step : (k + 1) * step], inverse, HIGHEST)
            rows[i] = with_column(rows[i], k, jnp.zeros((step, step), jnp.float32)) - jnp.dot(
                lower, rows[k], precision=HIGHEST, preferred_element_type=jnp.float32
            )
    return jnp.concatenate(rows, axis=0)


def gram_kernel(parts_ref, basis_ref, blocks_ref):
    basis = (parts_ref[0] + parts_ref[1]) + (parts_ref[2] + parts_ref[3])
    basis_ref[...] = basis
    gram = jnp.dot(basis.T, basis, precision=HIGHEST, preferred_element_type=jnp.float32)
    halves_of_row = gram.shape[1] // 128
    for block in range(blocks_ref.shape[0]):
        row, col = 8 * (block // halves_of_row), 128 * (block % halves_of_row)
        blocks_ref[block] = gram[row : row + 8, col : col + 128]


def copies_kernel(parts_ref, copies_ref):
    copies_ref[...] = jnp.broadcast_to(jnp.sum(parts_ref[...], axis=0)[None], copies_ref.shape)


def solve_kernel(blocks_ref, basis_ref, ortho_ref, *, share):
    size = basis_ref.shape[1]
    wide = size // 128
    gram = jnp.concatenate(
        [
            jnp.concatenate([blocks_ref[row * wide + part] for part in range(wide)], axis=1)
            for row in range(size // 8)
        ],
        axis=0,
    )
    source = lax.broadcasted_iota(jnp.int32, (size, size), 0)
    target = lax.broadcasted_iota(jnp.int32, (size, size), 1)
    diagonal = jnp.where(source == target, gram, 0.0)
    scale_row = lax.rsqrt(jnp.sum(diagonal, axis=0, keepdims=True))
    scale_column = lax.rsqrt(jnp.sum(diagonal, axis=1, keepdims=True))
    gram = gram * scale_column * scale_row
    inverse = inverse_factor(
        [gram[k : k + FACTOR_BLOCK] for k in range(0, size, FACTOR_BLOCK)]
    )
    inverse = jnp.where(source >= target, inverse * scale_row, 0.0)
    ortho = nt_dot(basis_ref[...], inverse, HIGHEST).astype(jnp.bfloat16)
    selection = (device_of(target // share) * share + target % share == source).astype(jnp.bfloat16)
    ortho_ref[...] = jnp.dot(ortho, selection, preferred_element_type=jnp.float32).astype(
        jnp.bfloat16
    )


VMEM = pl.BlockSpec(memory_space=pltpu.VMEM)


def local_call(kernel, name, shapes, *operands, scratch=(), flops=0):
    size = sum(math.prod(o.shape) * o.dtype.itemsize for o in operands)
    return pl.pallas_call(
        kernel,
        out_shape=shapes,
        in_specs=[VMEM] * len(operands),
        out_specs=jax.tree.map(lambda _: VMEM, shapes),
        scratch_shapes=scratch,
        compiler_params=pltpu.CompilerParams(vmem_limit_bytes=32 << 20),
        cost_estimate=pl.CostEstimate(flops=flops, bytes_accessed=2 * size, transcendentals=0),
        name=name,
    )(*operands)


def shaped(*shape, dtype=jnp.float32):
    return jax.ShapeDtypeStruct(shape, dtype)


def exchange(blocks, groups):
    return lax.all_to_all(blocks, AXES, 0, 0, axis_index_groups=groups, tiled=True)


def spread(block, groups):
    return exchange(jnp.broadcast_to(block[None], (len(groups[0]),) + block.shape), groups)


def spread_rows(block):
    return spread(spread(block, STRIDED), NEAR)


def add_up(blocks):
    parts = [blocks[i].astype(jnp.float32) for i in range(blocks.shape[0])]
    while len(parts) > 1:
        parts = [a + b for a, b in zip(parts[::2], parts[1::2])]
    return parts[0]


def device_of(place):
    parity, tile_index = place // 16, place % 16
    z = tile_index // 4 * 2 + parity // 2
    y = tile_index % 4 * 2 + parity % 2
    return z * SIDE + y


def nt_dot(a, b, precision=None):
    return lax.dot_general(
        a, b, (((1,), (1,)), ((), ())), precision=precision, preferred_element_type=jnp.float32
    )


def halves(block):
    middle = block.shape[1] // 2
    return jnp.concatenate([block[:, :middle], block[:, middle:]], axis=0)


def split_row(row, share):
    return row // (2 * share), row // share % 2, row % share


def exact_dot(a, selection):
    high = a.astype(jnp.bfloat16)
    rest = a - high.astype(jnp.float32)
    middle = rest.astype(jnp.bfloat16)
    low = (rest - middle.astype(jnp.float32)).astype(jnp.bfloat16)
    dot = functools.partial(jnp.dot, preferred_element_type=jnp.float32)
    return dot(high, selection) + (dot(middle, selection) + dot(low, selection))


def blend_kernel(momentum_ref, gradient_ref, blended_ref):
    blended_ref[...] = (
        momentum_ref[...].astype(jnp.float32) + gradient_ref[...].astype(jnp.float32)
    ).astype(jnp.bfloat16)


def basis_kernel(blended_ref, factor_ref, basis_ref, *, share):
    rows = blended_ref.shape[0]
    height, half = factor_ref.shape
    rank = height // 2
    place, _, low = split_row(lax.broadcasted_iota(jnp.int32, (height, rank), 0), share)
    target = lax.broadcasted_iota(jnp.int32, (height, rank), 1)
    selection = (device_of(place) * share + low == target).astype(jnp.bfloat16)
    _, part, _ = split_row(lax.broadcasted_iota(jnp.int32, (rows, height), 1), share)
    stacked = jnp.concatenate([blended_ref[:, :half], blended_ref[:, half:]], axis=0)
    products = nt_dot(stacked, factor_ref[...])
    basis_ref[...] = exact_dot(jnp.where(part == 0, products[:rows], products[rows:]), selection)


def momentum_kernel(ortho_ref, projection_ref, blended_ref, out_ref, left_ref, *, share):
    rows = ortho_ref.shape[0]
    height, half = projection_ref.shape
    rank = height // 2
    place, part, low = split_row(lax.broadcasted_iota(jnp.int32, (rank, height), 1), share)
    source = lax.broadcasted_iota(jnp.int32, (rank, height), 0)
    selection = (place * share + low == source).astype(jnp.bfloat16)
    left = jnp.dot(ortho_ref[...], selection, preferred_element_type=jnp.float32)
    part = part[0:1]
    left = jnp.concatenate([jnp.where(part == h, left, 0.0) for h in range(2)], axis=0)
    left = left.astype(jnp.bfloat16)
    left_ref[...] = left
    carried = jnp.dot(left, projection_ref[...], preferred_element_type=jnp.float32)
    for h in range(2):
        columns = slice(h * half, (h + 1) * half)
        out_ref[:, columns] = (
            blended_ref[:, columns].astype(jnp.float32)
            - (1.0 - MOMENTUM_DECAY) * carried[h * rows : (h + 1) * rows]
        ).astype(jnp.bfloat16)


def squares_kernel(projection_ref, copies_ref):
    height, half = projection_ref.shape
    sums = jnp.zeros((height, 128), jnp.float32)
    for column in range(0, half, 128):
        piece = projection_ref[:, column : column + 128].astype(jnp.float32)
        sums = sums + piece * piece
    totals = nt_dot(jnp.ones((8, 128), jnp.float32), sums, HIGHEST)
    copies_ref[...] = jnp.zeros(copies_ref.shape, jnp.float32)
    for copy in range(copies_ref.shape[0]):
        for piece in range(height // 128):
            copies_ref[copy, piece : piece + 1, :] = totals[0:1, piece * 128 : (piece + 1) * 128]


def update_kernel(left_ref, projection_ref, squares_ref, own_ref, out_ref, factor_ref, *, share, scale):
    height, half = projection_ref.shape
    pieces = jnp.sum(squares_ref[...], axis=0)
    squares = jnp.concatenate([pieces[i : i + 1] for i in range(height // 128)], axis=1)
    squares = jnp.broadcast_to(squares, (8, height))
    place, part, low = split_row(lax.broadcasted_iota(jnp.int32, (8, height), 1), share)
    other = jnp.where(
        part == 0, pltpu.roll(squares, height - share, 1), pltpu.roll(squares, share, 1)
    )
    inverse = 1.0 / (jnp.sqrt(squares + other) + EPSILON)
    left = (left_ref[...].astype(jnp.float32) * inverse[0:1]).astype(jnp.bfloat16)
    direction = jnp.dot(left, projection_ref[...], preferred_element_type=jnp.float32)
    rows = out_ref.shape[0]
    for h in range(2):
        out_ref[:, h * half : (h + 1) * half] = (
            scale * direction[h * rows : (h + 1) * rows]
        ).astype(jnp.bfloat16)
    mine = (device_of(place) == lax.axis_index("fsdp")) & (part == 0)
    mine = mine & (low == lax.broadcasted_iota(jnp.int32, (8, height), 0))
    own_inverse = jnp.sum(jnp.where(mine, inverse, 0.0), axis=1, keepdims=True)
    factor_ref[...] = own_ref[...] * own_inverse[0:share]


def body(momentum, gradient, right_factor):
    rows, cols = momentum.shape
    share = right_factor.shape[0]
    groups, columns = SIDE * SIDE, LINE * CORES
    tiles = groups // 4
    rank = share * groups
    with jax.named_scope("factor_gather"):
        blended = local_call(
            blend_kernel, "blended", shaped(rows, cols, dtype=jnp.bfloat16), momentum, gradient
        )
        strided = spread(halves(right_factor), STRIDED)
        strided, blended = lax.optimization_barrier((strided, blended))
        whole_factor = spread(strided, NEAR).reshape(2 * rank, cols // 2)
    with jax.named_scope("basis"):
        part = local_call(
            functools.partial(basis_kernel, share=share),
            "basis_part",
            shaped(rows, rank),
            blended, whole_factor,
        )
        other_core = [(i, i ^ 1) for i in range(columns)]
        parts = spread(part + lax.ppermute(part, "tp", other_core), ROW)
    with jax.named_scope("gram"):
        basis, blocks = local_call(
            gram_kernel,
            "gram_part",
            (shaped(rows, rank), shaped(groups, 8, rank * rank // groups // 8)),
            parts,
        )
        parts = exchange(blocks, PLANE)
        copies = local_call(copies_kernel, "gram_copies", shaped(*parts.shape), parts)
        blocks = exchange(copies, PLANE)
    with jax.named_scope("solve"):
        ortho_basis = local_call(
            functools.partial(solve_kernel, share=share),
            "ortho_basis",
            shaped(rows, rank, dtype=jnp.bfloat16),
            blocks, basis,
            flops=10**9,
        )
    with jax.named_scope("projection"):
        partial = lax.dot_general(
            ortho_basis, blended, (((0,), (0,)), ((), ())), preferred_element_type=jnp.float32
        ).astype(jnp.bfloat16)
        partial = exchange(partial.reshape(4, tiles * share, cols), NEAR)
        partial = add_up(partial).astype(jnp.bfloat16)
        partial = exchange(partial.reshape(tiles, share, cols), STRIDED)
        own = add_up(partial)
        projection = spread_rows(halves(own.astype(jnp.bfloat16))).reshape(2 * rank, cols // 2)
    with jax.named_scope("norms"):
        copies = local_call(squares_kernel, "squares", shaped(columns, 8, 128), projection)
        squares = exchange(copies, COLUMNS)
    with jax.named_scope("outputs"):
        momentum_next, left = local_call(
            functools.partial(momentum_kernel, share=share),
            "momentum_next",
            (shaped(rows, cols, dtype=jnp.bfloat16), shaped(2 * rows, 2 * rank, dtype=jnp.bfloat16)),
            ortho_basis, projection, blended,
            flops=8 * rows * cols * rank,
        )
        scale = math.sqrt(rows * groups * cols * columns / rank)
        update, factor_next = local_call(
            functools.partial(update_kernel, share=share, scale=scale),
            "update",
            (shaped(rows, cols, dtype=jnp.bfloat16), shaped(share, cols)),
            left, projection, squares, own,
            flops=8 * rows * cols * rank,
        )
    return (momentum_next, factor_next, update)


def solution(mesh):
    placed = P(*AXES)
    return jax.shard_map(
        body,
        mesh=mesh,
        in_specs=(placed, placed, placed),
        out_specs=(placed, placed, placed),
        check_vma=False,
    )
```

```python
import functools
import math

import jax
import jax.numpy as jnp
from jax import lax
from jax.experimental import pallas as pl
from jax.experimental.pallas import tpu as pltpu
from jax.sharding import PartitionSpec as P

EPSILON = 1e-06
MOMENTUM_DECAY = 0.95
HIGHEST = lax.Precision.HIGHEST

AXES = ("fsdp", "tp")
SIDE = 8
LINE = 4
CORES = 2


def groups_of(key, order):
    found = {}
    for index in range(SIDE * SIDE * LINE * CORES):
        fsdp, tp = divmod(index, LINE * CORES)
        place = divmod(fsdp, SIDE) + divmod(tp, CORES)
        found.setdefault(key(*place), []).append((order(*place), index))
    return [[index for _, index in sorted(group)] for group in found.values()]


def tile(place, core):
    return (place - core) % SIDE // 2


NEAR = groups_of(
    lambda z, y, x, core: (tile(z, core), tile(y, core), x, core), lambda z, y, x, core: (z % 2, y % 2)
)
STRIDED = groups_of(
    lambda z, y, x, core: (z % 2, y % 2, x, core), lambda z, y, x, core: (z // 2, y // 2)
)
FIRST_LINE = groups_of(
    lambda z, y, x, core: (z if core else y, x, core), lambda z, y, x, core: y if core else z
)
SECOND_LINE = groups_of(
    lambda z, y, x, core: (y if core else z, x, core), lambda z, y, x, core: z if core else y
)
COLUMNS = groups_of(lambda z, y, x, core: (z, y), lambda z, y, x, core: (x, core))
ROW = groups_of(lambda z, y, x, core: (z, y, core), lambda z, y, x, core: x)

FACTOR_BLOCK = 64
FACTOR_GROUP = 16


def block_inverse(block, size):
    sub = lax.broadcasted_iota(jnp.int32, (size, 128), 0)
    eye = (lax.broadcasted_iota(jnp.int32, (size, 128), 1) == sub + size).astype(jnp.float32)
    work = jnp.concatenate([block, jnp.zeros((size, 128 - size), jnp.float32)], axis=1) + eye
    done = []
    for start in range(0, size, FACTOR_GROUP):
        height = size - start
        sub = lax.broadcasted_iota(jnp.int32, (height, 128), 0)

        def row(array, index):
            return jnp.broadcast_to(array[index : index + 1, :], (height, 128))

        pivots = jnp.ones((height, 128), jnp.float32)
        columns = [
            jnp.broadcast_to(work[:, start + j : start + j + 1], (height, 128))
            for j in range(FACTOR_GROUP)
        ]
        for j in range(0, FACTOR_GROUP, 2):
            first, second = columns[j], columns[j + 1]
            a, e, b = row(first, j), row(first, j + 1), row(second, j + 1)
            det = a * b - e * e
            inverse_det, inverse_a = 1.0 / det, 1.0 / a
            ratio = jnp.where(sub > j + 1, (first * b - second * e) * inverse_det, 0.0)
            ratio = jnp.where(sub == j + 1, e * inverse_a, ratio)
            other = jnp.where(sub > j + 1, (second * a - first * e) * inverse_det, 0.0)
            pivots = jnp.where(sub == j, a, jnp.where(sub == j + 1, det * inverse_a, pivots))
            for later in range(j + 2, FACTOR_GROUP):
                column = columns[later]
                columns[later] = column - ratio * row(column, j) - other * row(column, j + 1)
            work = work - ratio * row(work, j) - other * row(work, j + 1)
        done.append(work[:FACTOR_GROUP] * lax.rsqrt(pivots[:FACTOR_GROUP]))
        work = work[FACTOR_GROUP:]
    return jnp.concatenate(done, axis=0)[:, size : 2 * size]


def inverse_factor(rows):
    step = FACTOR_BLOCK
    rows = list(rows)
    count = len(rows)

    def with_column(row, k, block):
        pieces = [row[:, q * step : (q + 1) * step] for q in range(count)]
        return jnp.concatenate(pieces[:k] + [block] + pieces[k + 1 :], axis=1)

    for k in range(count):
        inverse = block_inverse(rows[k][:, k * step : (k + 1) * step], step)
        panel = jnp.dot(inverse, rows[k], precision=HIGHEST, preferred_element_type=jnp.float32)
        rows[k] = with_column(panel, k, inverse)
        for i in range(k + 1, count):
            lower = nt_dot(rows[i][:, k * step : (k + 1) * step], inverse, HIGHEST)
            rows[i] = with_column(rows[i], k, jnp.zeros((step, step), jnp.float32)) - jnp.dot(
                lower, rows[k], precision=HIGHEST, preferred_element_type=jnp.float32
            )
    return jnp.concatenate(rows, axis=0)


def gram_kernel(parts_ref, basis_ref, copies_ref, gram_ref):
    basis = (parts_ref[0] + parts_ref[1]) + (parts_ref[2] + parts_ref[3])
    basis_ref[...] = basis
    half = basis.shape[1] // 2
    turned = basis.T
    left = jnp.dot(
        turned, basis[:, :half], precision=HIGHEST, preferred_element_type=jnp.float32
    )
    right = jnp.dot(
        turned[half:], basis[:, half:], precision=HIGHEST, preferred_element_type=jnp.float32
    )
    gram_ref[0 : 2 * half, :] = left
    gram_ref[2 * half :, :] = right
    share = half // copies_ref.shape[0]
    first = pl.multiple_of(lax.axis_index("tp") * share, share)
    for quarter in range(3):
        piece = gram_ref[pl.ds(quarter * half + first, share), :]
        copies_ref[:, quarter * share : (quarter + 1) * share, :] = jnp.broadcast_to(
            piece[None], (copies_ref.shape[0],) + piece.shape
        )


def copies_kernel(parts_ref, copies_ref):
    copies_ref[...] = jnp.broadcast_to(jnp.sum(parts_ref[...], axis=0)[None], copies_ref.shape)


def solve_kernel(blocks_ref, basis_ref, ortho_ref, *, share):
    size = basis_ref.shape[1]
    height = blocks_ref.shape[1] // 3
    upper, lower, corner = [
        jnp.concatenate(
            [blocks_ref[t, q * height : (q + 1) * height] for t in range(blocks_ref.shape[0])], axis=0
        )
        for q in range(3)
    ]
    gram = jnp.concatenate(
        [jnp.concatenate([upper, lower.T], axis=1), jnp.concatenate([lower, corner], axis=1)], axis=0
    )
    source = lax.broadcasted_iota(jnp.int32, (size, size), 0)
    target = lax.broadcasted_iota(jnp.int32, (size, size), 1)
    diagonal = jnp.where(source == target, gram, 0.0)
    scale_row = lax.rsqrt(jnp.sum(diagonal, axis=0, keepdims=True))
    scale_column = lax.rsqrt(jnp.sum(diagonal, axis=1, keepdims=True))
    gram = gram * scale_column * scale_row
    inverse = inverse_factor(
        [gram[k : k + FACTOR_BLOCK] for k in range(0, size, FACTOR_BLOCK)]
    )
    inverse = jnp.where(source >= target, inverse * scale_row, 0.0)
    ortho = nt_dot(basis_ref[...], inverse, HIGHEST).astype(jnp.bfloat16)
    selection = (device_of(target // share) * share + target % share == source).astype(jnp.bfloat16)
    ortho_ref[...] = jnp.dot(ortho, selection, preferred_element_type=jnp.float32).astype(
        jnp.bfloat16
    )


VMEM = pl.BlockSpec(memory_space=pltpu.VMEM)


def local_call(kernel, name, shapes, *operands, scratch=(), flops=0):
    size = sum(math.prod(o.shape) * o.dtype.itemsize for o in operands)
    return pl.pallas_call(
        kernel,
        out_shape=shapes,
        in_specs=[VMEM] * len(operands),
        out_specs=jax.tree.map(lambda _: VMEM, shapes),
        scratch_shapes=scratch,
        compiler_params=pltpu.CompilerParams(vmem_limit_bytes=32 << 20),
        cost_estimate=pl.CostEstimate(flops=flops, bytes_accessed=2 * size, transcendentals=0),
        name=name,
    )(*operands)


def shaped(*shape, dtype=jnp.float32):
    return jax.ShapeDtypeStruct(shape, dtype)


def exchange(blocks, groups):
    return lax.all_to_all(blocks, AXES, 0, 0, axis_index_groups=groups, tiled=True)


def spread(block, groups):
    return exchange(jnp.broadcast_to(block[None], (len(groups[0]),) + block.shape), groups)


def add_up(blocks):
    parts = [blocks[i].astype(jnp.float32) for i in range(blocks.shape[0])]
    while len(parts) > 1:
        parts = [a + b for a, b in zip(parts[::2], parts[1::2])]
    return parts[0]


def device_of(place):
    parity, tile_index = place // 16, place % 16
    z = tile_index // 4 * 2 + parity // 2
    y = tile_index % 4 * 2 + parity % 2
    return z * SIDE + y


def nt_dot(a, b, precision=None):
    return lax.dot_general(
        a, b, (((1,), (1,)), ((), ())), precision=precision, preferred_element_type=jnp.float32
    )


def halves(block):
    middle = block.shape[1] // 2
    return jnp.concatenate([block[:, :middle], block[:, middle:]], axis=0)


def split_row(row, share):
    return row // (2 * share), row // share % 2, row % share


def exact_dot(a, selection):
    high = a.astype(jnp.bfloat16)
    rest = a - high.astype(jnp.float32)
    middle = rest.astype(jnp.bfloat16)
    low = (rest - middle.astype(jnp.float32)).astype(jnp.bfloat16)
    dot = functools.partial(jnp.dot, preferred_element_type=jnp.float32)
    return dot(high, selection) + (dot(middle, selection) + dot(low, selection))


def basis_kernel(momentum_ref, gradient_ref, factor_ref, blended_ref, basis_ref, *, share):
    blended_ref[...] = (
        momentum_ref[...].astype(jnp.float32) + gradient_ref[...].astype(jnp.float32)
    ).astype(jnp.bfloat16)
    rows = blended_ref.shape[0]
    height, half = factor_ref.shape
    rank = height // 2
    place, _, low = split_row(lax.broadcasted_iota(jnp.int32, (height, rank), 0), share)
    target = lax.broadcasted_iota(jnp.int32, (height, rank), 1)
    selection = (device_of(place) * share + low == target).astype(jnp.bfloat16)
    _, part, _ = split_row(lax.broadcasted_iota(jnp.int32, (rows, height), 1), share)
    stacked = jnp.concatenate([blended_ref[:, :half], blended_ref[:, half:]], axis=0)
    products = nt_dot(stacked, factor_ref[...])
    basis_ref[...] = exact_dot(jnp.where(part == 0, products[:rows], products[rows:]), selection)


def momentum_kernel(ortho_ref, projection_ref, blended_ref, out_ref, left_ref, *, share):
    rows = ortho_ref.shape[0]
    height, half = projection_ref.shape
    rank = height // 2
    place, part, low = split_row(lax.broadcasted_iota(jnp.int32, (rank, height), 1), share)
    source = lax.broadcasted_iota(jnp.int32, (rank, height), 0)
    selection = (place * share + low == source).astype(jnp.bfloat16)
    left = jnp.dot(ortho_ref[...], selection, preferred_element_type=jnp.float32)
    part = part[0:1]
    left = jnp.concatenate([jnp.where(part == h, left, 0.0) for h in range(2)], axis=0)
    left = left.astype(jnp.bfloat16)
    left_ref[...] = left
    carried = jnp.dot(left, projection_ref[...], preferred_element_type=jnp.float32)
    for h in range(2):
        columns = slice(h * half, (h + 1) * half)
        out_ref[:, columns] = (
            blended_ref[:, columns].astype(jnp.float32)
            - (1.0 - MOMENTUM_DECAY) * carried[h * rows : (h + 1) * rows]
        ).astype(jnp.bfloat16)


def squares_kernel(projection_ref, copies_ref):
    height, half = projection_ref.shape
    sums = jnp.zeros((height, 128), jnp.float32)
    for column in range(0, half, 128):
        piece = projection_ref[:, column : column + 128].astype(jnp.float32)
        sums = sums + piece * piece
    totals = jnp.sum(sums.T, axis=0, keepdims=True)
    copies_ref[...] = jnp.zeros(copies_ref.shape, jnp.float32)
    for copy in range(copies_ref.shape[0]):
        for piece in range(height // 128):
            copies_ref[copy, piece : piece + 1, :] = totals[0:1, piece * 128 : (piece + 1) * 128]


def update_kernel(left_ref, projection_ref, squares_ref, own_ref, out_ref, factor_ref, *, share, scale):
    height, half = projection_ref.shape
    pieces = jnp.sum(squares_ref[...], axis=0)
    squares = jnp.concatenate([pieces[i : i + 1] for i in range(height // 128)], axis=1)
    squares = jnp.broadcast_to(squares, (8, height))
    place, part, low = split_row(lax.broadcasted_iota(jnp.int32, (8, height), 1), share)
    other = jnp.where(
        part == 0, pltpu.roll(squares, height - share, 1), pltpu.roll(squares, share, 1)
    )
    inverse = 1.0 / (jnp.sqrt(squares + other) + EPSILON)
    left = (left_ref[...].astype(jnp.float32) * inverse[0:1]).astype(jnp.bfloat16)
    direction = jnp.dot(left, projection_ref[...], preferred_element_type=jnp.float32)
    rows = out_ref.shape[0]
    for h in range(2):
        out_ref[:, h * half : (h + 1) * half] = (
            scale * direction[h * rows : (h + 1) * rows]
        ).astype(jnp.bfloat16)
    mine = (device_of(place) == lax.axis_index("fsdp")) & (part == 0)
    mine = mine & (low == lax.broadcasted_iota(jnp.int32, (8, height), 0))
    own_inverse = jnp.sum(jnp.where(mine, inverse, 0.0), axis=1, keepdims=True)
    factor_ref[...] = own_ref[...] * own_inverse[0:share]


def body(momentum, gradient, right_factor):
    rows, cols = momentum.shape
    share = right_factor.shape[0]
    groups, columns = SIDE * SIDE, LINE * CORES
    tiles = groups // 4
    rank = share * groups
    with jax.named_scope("factor_gather"):
        whole_factor = spread(spread(halves(right_factor), STRIDED), NEAR)
        whole_factor = whole_factor.reshape(2 * rank, cols // 2)
    with jax.named_scope("basis"):
        blended, part = local_call(
            functools.partial(basis_kernel, share=share),
            "basis_part",
            (shaped(rows, cols, dtype=jnp.bfloat16), shaped(rows, rank)),
            momentum, gradient, whole_factor,
        )
        other_core = [(i, i ^ 1) for i in range(columns)]
        parts = spread(part + lax.ppermute(part, "tp", other_core), ROW)
    with jax.named_scope("gram"):
        shape = (columns, 3 * rank // 2 // columns, rank // 2)
        basis, copies = local_call(
            gram_kernel,
            "gram_part",
            (shaped(rows, rank), shaped(*shape)),
            parts,
            scratch=[pltpu.VMEM((3 * rank // 2, rank // 2), jnp.float32)],
        )
        copies = local_call(copies_kernel, "gram_first", shaped(*shape), exchange(copies, FIRST_LINE))
        copies = local_call(copies_kernel, "gram_second", shaped(*shape), exchange(copies, SECOND_LINE))
        blocks = exchange(copies, COLUMNS)
    with jax.named_scope("solve"):
        ortho_basis = local_call(
            functools.partial(solve_kernel, share=share),
            "ortho_basis",
            shaped(rows, rank, dtype=jnp.bfloat16),
            blocks, basis,
            flops=10**9,
        )
    with jax.named_scope("projection"):
        partial = lax.dot_general(
            ortho_basis, blended, (((0,), (0,)), ((), ())), preferred_element_type=jnp.float32
        ).astype(jnp.bfloat16)
        partial = exchange(partial.reshape(4, tiles * share, cols), NEAR)
        partial = add_up(partial).astype(jnp.bfloat16)
        partial = exchange(partial.reshape(tiles, share, cols), STRIDED)
        own = add_up(partial)
        projection = spread(spread(halves(own.astype(jnp.bfloat16)), STRIDED), NEAR)
        projection = projection.reshape(2 * rank, cols // 2)
    with jax.named_scope("norms"):
        copies = local_call(squares_kernel, "squares", shaped(columns, 8, 128), projection)
        squares = exchange(copies, COLUMNS)
    with jax.named_scope("outputs"):
        momentum_next, left = local_call(
            functools.partial(momentum_kernel, share=share),
            "momentum_next",
            (shaped(rows, cols, dtype=jnp.bfloat16), shaped(2 * rows, 2 * rank, dtype=jnp.bfloat16)),
            ortho_basis, projection, blended,
            flops=8 * rows * cols * rank,
        )
        scale = math.sqrt(rows * groups * cols * columns / rank)
        update, factor_next = local_call(
            functools.partial(update_kernel, share=share, scale=scale),
            "update",
            (shaped(rows, cols, dtype=jnp.bfloat16), shaped(share, cols)),
            left, projection, squares, own,
            flops=8 * rows * cols * rank,
        )
    return (momentum_next, factor_next, update)


def solution(mesh):
    placed = P(*AXES)
    return jax.shard_map(
        body,
        mesh=mesh,
        in_specs=(placed, placed, placed),
        out_specs=(placed, placed, placed),
        check_vma=False,
    )
```

```python
import functools
import math

import jax
import jax.numpy as jnp
from jax import lax
from jax.experimental import pallas as pl
from jax.experimental.pallas import tpu as pltpu
from jax.sharding import PartitionSpec as P

EPSILON = 1e-06
MOMENTUM_DECAY = 0.95
HIGHEST = lax.Precision.HIGHEST

AXES = ("fsdp", "tp")
SIDE = 8
LINE = 4
CORES = 2


def groups_of(key, order):
    found = {}
    for index in range(SIDE * SIDE * LINE * CORES):
        fsdp, tp = divmod(index, LINE * CORES)
        place = divmod(fsdp, SIDE) + divmod(tp, CORES)
        found.setdefault(key(*place), []).append((order(*place), index))
    return [[index for _, index in sorted(group)] for group in found.values()]


def tile(place, core):
    return (place - core) % SIDE // 2


NEAR = groups_of(
    lambda z, y, x, core: (tile(z, core), tile(y, core), x, core), lambda z, y, x, core: (z % 2, y % 2)
)
STRIDED = groups_of(
    lambda z, y, x, core: (z % 2, y % 2, x, core), lambda z, y, x, core: (z // 2, y // 2)
)
SPARSE_FIRST = groups_of(
    lambda z, y, x, core: (z, y % 2, x, core) if core else (z % 2, y, x, core),
    lambda z, y, x, core: y if core else z,
)
SPARSE_SECOND = groups_of(
    lambda z, y, x, core: (z % 2, y, x, core) if core else (z, y % 2, x, core),
    lambda z, y, x, core: z if core else y,
)
FIRST_LINE = groups_of(
    lambda z, y, x, core: (z if core else y, x, core), lambda z, y, x, core: y if core else z
)
SECOND_LINE = groups_of(
    lambda z, y, x, core: (y if core else z, x, core), lambda z, y, x, core: z if core else y
)
COLUMNS = groups_of(lambda z, y, x, core: (z, y), lambda z, y, x, core: (x, core))
ROW = groups_of(lambda z, y, x, core: (z, y, core), lambda z, y, x, core: x)

FACTOR_BLOCK = 64
FACTOR_GROUP = 16


def block_inverse(block, size):
    sub = lax.broadcasted_iota(jnp.int32, (size, 128), 0)
    eye = (lax.broadcasted_iota(jnp.int32, (size, 128), 1) == sub + size).astype(jnp.float32)
    work = jnp.concatenate([block, jnp.zeros((size, 128 - size), jnp.float32)], axis=1) + eye
    done = []
    for start in range(0, size, FACTOR_GROUP):
        height = size - start
        sub = lax.broadcasted_iota(jnp.int32, (height, 128), 0)

        def row(array, index):
            return jnp.broadcast_to(array[index : index + 1, :], (height, 128))

        pivots = jnp.ones((height, 128), jnp.float32)
        columns = [
            jnp.broadcast_to(work[:, start + j : start + j + 1], (height, 128))
            for j in range(FACTOR_GROUP)
        ]
        for j in range(0, FACTOR_GROUP, 2):
            first, second = columns[j], columns[j + 1]
            a, e, b = row(first, j), row(first, j + 1), row(second, j + 1)
            det = a * b - e * e
            inverse_det, inverse_a = 1.0 / det, 1.0 / a
            ratio = jnp.where(sub > j + 1, (first * b - second * e) * inverse_det, 0.0)
            ratio = jnp.where(sub == j + 1, e * inverse_a, ratio)
            other = jnp.where(sub > j + 1, (second * a - first * e) * inverse_det, 0.0)
            pivots = jnp.where(sub == j, a, jnp.where(sub == j + 1, det * inverse_a, pivots))
            for later in range(j + 2, FACTOR_GROUP):
                column = columns[later]
                columns[later] = column - ratio * row(column, j) - other * row(column, j + 1)
            work = work - ratio * row(work, j) - other * row(work, j + 1)
        done.append(work[:FACTOR_GROUP] * lax.rsqrt(pivots[:FACTOR_GROUP]))
        work = work[FACTOR_GROUP:]
    return jnp.concatenate(done, axis=0)[:, size : 2 * size]


def inverse_factor(rows):
    step = FACTOR_BLOCK
    rows = list(rows)
    count = len(rows)

    def with_column(row, k, block):
        pieces = [row[:, q * step : (q + 1) * step] for q in range(count)]
        return jnp.concatenate(pieces[:k] + [block] + pieces[k + 1 :], axis=1)

    for k in range(count):
        inverse = block_inverse(rows[k][:, k * step : (k + 1) * step], step)
        panel = jnp.dot(inverse, rows[k], precision=HIGHEST, preferred_element_type=jnp.float32)
        rows[k] = with_column(panel, k, inverse)
        for i in range(k + 1, count):
            lower = nt_dot(rows[i][:, k * step : (k + 1) * step], inverse, HIGHEST)
            rows[i] = with_column(rows[i], k, jnp.zeros((step, step), jnp.float32)) - jnp.dot(
                lower, rows[k], precision=HIGHEST, preferred_element_type=jnp.float32
            )
    return jnp.concatenate(rows, axis=0)


def gram_kernel(parts_ref, basis_ref, copies_ref, gram_ref):
    basis = (parts_ref[0] + parts_ref[1]) + (parts_ref[2] + parts_ref[3])
    basis_ref[...] = basis
    half = basis.shape[1] // 2
    turned = basis.T
    left = jnp.dot(
        turned, basis[:, :half], precision=HIGHEST, preferred_element_type=jnp.float32
    )
    right = jnp.dot(
        turned[half:], basis[:, half:], precision=HIGHEST, preferred_element_type=jnp.float32
    )
    gram_ref[0 : 2 * half, :] = left
    gram_ref[2 * half :, :] = right
    share = half // copies_ref.shape[0]
    first = pl.multiple_of(lax.axis_index("tp") * share, share)
    for quarter in range(3):
        piece = gram_ref[pl.ds(quarter * half + first, share), :]
        copies_ref[:, quarter * share : (quarter + 1) * share, :] = jnp.broadcast_to(
            piece[None], (copies_ref.shape[0],) + piece.shape
        )


def copies_kernel(parts_ref, copies_ref):
    copies_ref[...] = jnp.broadcast_to(jnp.sum(parts_ref[...], axis=0)[None], copies_ref.shape)


def solve_kernel(blocks_ref, basis_ref, ortho_ref, *, share):
    size = basis_ref.shape[1]
    height = blocks_ref.shape[1] // 3
    upper, lower, corner = [
        jnp.concatenate(
            [blocks_ref[t, q * height : (q + 1) * height] for t in range(blocks_ref.shape[0])], axis=0
        )
        for q in range(3)
    ]
    gram = jnp.concatenate(
        [jnp.concatenate([upper, lower.T], axis=1), jnp.concatenate([lower, corner], axis=1)], axis=0
    )
    source = lax.broadcasted_iota(jnp.int32, (size, size), 0)
    target = lax.broadcasted_iota(jnp.int32, (size, size), 1)
    diagonal = jnp.where(source == target, gram, 0.0)
    scale_row = lax.rsqrt(jnp.sum(diagonal, axis=0, keepdims=True))
    scale_column = lax.rsqrt(jnp.sum(diagonal, axis=1, keepdims=True))
    gram = gram * scale_column * scale_row
    inverse = inverse_factor(
        [gram[k : k + FACTOR_BLOCK] for k in range(0, size, FACTOR_BLOCK)]
    )
    inverse = jnp.where(source >= target, inverse * scale_row, 0.0)
    ortho = nt_dot(basis_ref[...], inverse, HIGHEST).astype(jnp.bfloat16)
    rank_of = device_of(target // share, second_core()) * share + target % share
    selection = (rank_of == source).astype(jnp.bfloat16)
    ortho_ref[...] = jnp.dot(ortho, selection, preferred_element_type=jnp.float32).astype(
        jnp.bfloat16
    )


VMEM = pl.BlockSpec(memory_space=pltpu.VMEM)


def local_call(kernel, name, shapes, *operands, scratch=(), flops=0):
    size = sum(math.prod(o.shape) * o.dtype.itemsize for o in operands)
    return pl.pallas_call(
        kernel,
        out_shape=shapes,
        in_specs=[VMEM] * len(operands),
        out_specs=jax.tree.map(lambda _: VMEM, shapes),
        scratch_shapes=scratch,
        compiler_params=pltpu.CompilerParams(vmem_limit_bytes=32 << 20),
        cost_estimate=pl.CostEstimate(flops=flops, bytes_accessed=2 * size, transcendentals=0),
        name=name,
    )(*operands)


def shaped(*shape, dtype=jnp.float32):
    return jax.ShapeDtypeStruct(shape, dtype)


def exchange(blocks, groups):
    return lax.all_to_all(blocks, AXES, 0, 0, axis_index_groups=groups, tiled=True)


def spread(block, groups):
    return exchange(jnp.broadcast_to(block[None], (len(groups[0]),) + block.shape), groups)


def add_up(blocks):
    parts = [blocks[i].astype(jnp.float32) for i in range(blocks.shape[0])]
    while len(parts) > 1:
        parts = [a + b for a, b in zip(parts[::2], parts[1::2])]
    return parts[0]


def device_of(place, swapped=False):
    parity, first, second = place // 16, place // 4 % 4, place % 4
    z = jnp.where(swapped, second, first) * 2 + parity // 2
    y = jnp.where(swapped, first, second) * 2 + parity % 2
    return z * SIDE + y


def second_core():
    return lax.rem(lax.axis_index("tp"), CORES) == 1


def nt_dot(a, b, precision=None):
    return lax.dot_general(
        a, b, (((1,), (1,)), ((), ())), precision=precision, preferred_element_type=jnp.float32
    )


def halves(block):
    middle = block.shape[1] // 2
    return jnp.concatenate([block[:, :middle], block[:, middle:]], axis=0)


def split_row(row, share):
    return row // (2 * share), row // share % 2, row % share


def exact_dot(a, selection):
    high = a.astype(jnp.bfloat16)
    rest = a - high.astype(jnp.float32)
    middle = rest.astype(jnp.bfloat16)
    low = (rest - middle.astype(jnp.float32)).astype(jnp.bfloat16)
    dot = functools.partial(jnp.dot, preferred_element_type=jnp.float32)
    return dot(high, selection) + (dot(middle, selection) + dot(low, selection))


def basis_kernel(momentum_ref, gradient_ref, factor_ref, blended_ref, basis_ref, *, share):
    blended_ref[...] = (
        momentum_ref[...].astype(jnp.float32) + gradient_ref[...].astype(jnp.float32)
    ).astype(jnp.bfloat16)
    rows = blended_ref.shape[0]
    height, half = factor_ref.shape
    rank = height // 2
    place, _, low = split_row(lax.broadcasted_iota(jnp.int32, (height, rank), 0), share)
    target = lax.broadcasted_iota(jnp.int32, (height, rank), 1)
    selection = (device_of(place) * share + low == target).astype(jnp.bfloat16)
    _, part, _ = split_row(lax.broadcasted_iota(jnp.int32, (rows, height), 1), share)
    stacked = jnp.concatenate([blended_ref[:, :half], blended_ref[:, half:]], axis=0)
    products = nt_dot(stacked, factor_ref[...])
    basis_ref[...] = exact_dot(jnp.where(part == 0, products[:rows], products[rows:]), selection)


def momentum_kernel(ortho_ref, projection_ref, blended_ref, out_ref, left_ref, *, share):
    rows = ortho_ref.shape[0]
    height, half = projection_ref.shape
    rank = height // 2
    place, part, low = split_row(lax.broadcasted_iota(jnp.int32, (rank, height), 1), share)
    source = lax.broadcasted_iota(jnp.int32, (rank, height), 0)
    selection = (place * share + low == source).astype(jnp.bfloat16)
    left = jnp.dot(ortho_ref[...], selection, preferred_element_type=jnp.float32)
    part = part[0:1]
    left = jnp.concatenate([jnp.where(part == h, left, 0.0) for h in range(2)], axis=0)
    left = left.astype(jnp.bfloat16)
    left_ref[...] = left
    carried = jnp.dot(left, projection_ref[...], preferred_element_type=jnp.float32)
    for h in range(2):
        columns = slice(h * half, (h + 1) * half)
        out_ref[:, columns] = (
            blended_ref[:, columns].astype(jnp.float32)
            - (1.0 - MOMENTUM_DECAY) * carried[h * rows : (h + 1) * rows]
        ).astype(jnp.bfloat16)


def squares_kernel(projection_ref, copies_ref):
    height, half = projection_ref.shape
    sums = jnp.zeros((height, 128), jnp.float32)
    for column in range(0, half, 128):
        piece = projection_ref[:, column : column + 128].astype(jnp.float32)
        sums = sums + piece * piece
    totals = jnp.sum(sums.T, axis=0, keepdims=True)
    copies_ref[...] = jnp.zeros(copies_ref.shape, jnp.float32)
    for copy in range(copies_ref.shape[0]):
        for piece in range(height // 128):
            copies_ref[copy, piece : piece + 1, :] = totals[0:1, piece * 128 : (piece + 1) * 128]


def swap_lines(pieces, share):
    lane = lax.broadcasted_iota(jnp.int32, pieces.shape, 1)
    count = SIDE // 2
    outer = 2 * count * share
    distance = lane // outer - lane // share % count
    result = jnp.where(distance == 0, pieces, 0.0)
    for step in range(1 - count, count):
        if step:
            moved = pltpu.roll(pieces, step * (outer - share) % 128, 1)
            result = jnp.where(distance == step, moved, result)
    return result


def update_kernel(
    left_ref, projection_ref, squares_ref, sums_ref, out_ref, factor_ref, *, share, scale
):
    height, half = projection_ref.shape
    swapped = second_core()
    first = jnp.sum(jnp.stack([squares_ref[t] for t in range(0, LINE * CORES, 2)]), axis=0)
    second = jnp.sum(jnp.stack([squares_ref[t] for t in range(1, LINE * CORES, 2)]), axis=0)
    pieces = jnp.where(swapped, second, first) + swap_lines(
        jnp.where(swapped, first, second), factor_ref.shape[0]
    )
    squares = jnp.concatenate([pieces[i : i + 1] for i in range(height // 128)], axis=1)
    squares = jnp.broadcast_to(squares, (8, height))
    place, part, low = split_row(lax.broadcasted_iota(jnp.int32, (8, height), 1), share)
    other = jnp.where(
        part == 0, pltpu.roll(squares, height - share, 1), pltpu.roll(squares, share, 1)
    )
    inverse = 1.0 / (jnp.sqrt(squares + other) + EPSILON)
    left = (left_ref[...].astype(jnp.float32) * inverse[0:1]).astype(jnp.bfloat16)
    direction = jnp.dot(left, projection_ref[...], preferred_element_type=jnp.float32)
    rows = out_ref.shape[0]
    for h in range(2):
        out_ref[:, h * half : (h + 1) * half] = (
            scale * direction[h * rows : (h + 1) * rows]
        ).astype(jnp.bfloat16)
    own_share, device = factor_ref.shape[0], lax.axis_index("fsdp")
    mine = device_of(place * (share // own_share) + low // own_share, swapped) == device
    row = lax.broadcasted_iota(jnp.int32, (8, height), 0)
    mine = mine & (part == 0) & (low % own_share == row)
    own_inverse = jnp.sum(jnp.where(mine, inverse, 0.0), axis=1, keepdims=True)
    own_line = jnp.where(swapped, lax.div(device, SIDE), lax.rem(device, SIDE))
    own = jnp.zeros(factor_ref.shape, jnp.float32)
    for block in range(share // own_share):
        rows_of_block = sums_ref[block * own_share : (block + 1) * own_share, :]
        own = jnp.where(lax.div(own_line, 2) == block, rows_of_block, own)
    factor_ref[...] = own * own_inverse[0:own_share]


def body(momentum, gradient, right_factor):
    rows, cols = momentum.shape
    share = right_factor.shape[0]
    groups, columns = SIDE * SIDE, LINE * CORES
    tiles = groups // 4
    rank = share * groups
    with jax.named_scope("factor_gather"):
        whole_factor = spread(spread(halves(right_factor), STRIDED), NEAR)
        whole_factor = whole_factor.reshape(2 * rank, cols // 2)
    with jax.named_scope("basis"):
        blended, part = local_call(
            functools.partial(basis_kernel, share=share),
            "basis_part",
            (shaped(rows, cols, dtype=jnp.bfloat16), shaped(rows, rank)),
            momentum, gradient, whole_factor,
        )
        other_core = [(i, i ^ 1) for i in range(columns)]
        parts = spread(part + lax.ppermute(part, "tp", other_core), ROW)
    with jax.named_scope("gram"):
        shape = (columns, 3 * rank // 2 // columns, rank // 2)
        basis, copies = local_call(
            gram_kernel,
            "gram_part",
            (shaped(rows, rank), shaped(*shape)),
            parts,
            scratch=[pltpu.VMEM((3 * rank // 2, rank // 2), jnp.float32)],
        )
        copies = local_call(copies_kernel, "gram_first", shaped(*shape), exchange(copies, FIRST_LINE))
        copies = local_call(copies_kernel, "gram_second", shaped(*shape), exchange(copies, SECOND_LINE))
        blocks = exchange(copies, COLUMNS)
    with jax.named_scope("solve"):
        ortho_basis = local_call(
            functools.partial(solve_kernel, share=share),
            "ortho_basis",
            shaped(rows, rank, dtype=jnp.bfloat16),
            blocks, basis,
            flops=10**9,
        )
    with jax.named_scope("projection"):
        partial = lax.dot_general(
            ortho_basis, blended, (((0,), (0,)), ((), ())), preferred_element_type=jnp.float32
        ).astype(jnp.bfloat16)
        partial = exchange(partial.reshape(4, tiles * share, cols), NEAR)
        partial = add_up(partial).astype(jnp.bfloat16)
        lines = SIDE // 2
        partial = exchange(partial.reshape(lines, lines * share, cols), SPARSE_FIRST)
        partial = spread(add_up(partial).astype(jnp.bfloat16), SPARSE_SECOND)
        sums = add_up(partial)
        strided = spread(halves(sums.astype(jnp.bfloat16)), SPARSE_FIRST)
        projection = spread(strided, NEAR).reshape(2 * rank, cols // 2)
    with jax.named_scope("norms"):
        copies = local_call(squares_kernel, "squares", shaped(columns, 8, 128), projection)
        squares = exchange(copies, COLUMNS)
    with jax.named_scope("outputs"):
        momentum_next, left = local_call(
            functools.partial(momentum_kernel, share=lines * share),
            "momentum_next",
            (shaped(rows, cols, dtype=jnp.bfloat16), shaped(2 * rows, 2 * rank, dtype=jnp.bfloat16)),
            ortho_basis, projection, blended,
            flops=8 * rows * cols * rank,
        )
        scale = math.sqrt(rows * groups * cols * columns / rank)
        update, factor_next = local_call(
            functools.partial(update_kernel, share=lines * share, scale=scale),
            "update",
            (shaped(rows, cols, dtype=jnp.bfloat16), shaped(share, cols)),
            left, projection, squares, sums,
            flops=8 * rows * cols * rank,
        )
    return (momentum_next, factor_next, update)


def solution(mesh):
    placed = P(*AXES)
    return jax.shard_map(
        body,
        mesh=mesh,
        in_specs=(placed, placed, placed),
        out_specs=(placed, placed, placed),
        check_vma=False,
    )
```

```python
import functools
import math

import jax
import jax.numpy as jnp
from jax import lax
from jax.experimental import pallas as pl
from jax.experimental.pallas import tpu as pltpu
from jax.sharding import PartitionSpec as P

EPSILON = 1e-06
MOMENTUM_DECAY = 0.95
HIGHEST = lax.Precision.HIGHEST

AXES = ("fsdp", "tp")
SIDE = 8
LINE = 4
CORES = 2


def groups_of(key, order):
    found = {}
    for index in range(SIDE * SIDE * LINE * CORES):
        fsdp, tp = divmod(index, LINE * CORES)
        place = divmod(fsdp, SIDE) + divmod(tp, CORES)
        found.setdefault(key(*place), []).append((order(*place), index))
    return [[index for _, index in sorted(group)] for group in found.values()]


def tile(place, core):
    return (place - core) % SIDE // 2


NEAR = groups_of(
    lambda z, y, x, core: (tile(z, core), tile(y, core), x, core), lambda z, y, x, core: (z % 2, y % 2)
)
STRIDED = groups_of(
    lambda z, y, x, core: (z % 2, y % 2, x, core), lambda z, y, x, core: (z // 2, y // 2)
)
SPARSE_FIRST = groups_of(
    lambda z, y, x, core: (z, y % 2, x, core) if core else (z % 2, y, x, core),
    lambda z, y, x, core: y if core else z,
)
SPARSE_SECOND = groups_of(
    lambda z, y, x, core: (z % 2, y, x, core) if core else (z, y % 2, x, core),
    lambda z, y, x, core: z if core else y,
)
FIRST_LINE = groups_of(
    lambda z, y, x, core: (z if core else y, x, core), lambda z, y, x, core: y if core else z
)
SECOND_LINE = groups_of(
    lambda z, y, x, core: (y if core else z, x, core), lambda z, y, x, core: z if core else y
)
COLUMNS = groups_of(lambda z, y, x, core: (z, y), lambda z, y, x, core: (x, core))
ROW = groups_of(lambda z, y, x, core: (z, y, core), lambda z, y, x, core: x)

FACTOR_BLOCK = 64
FACTOR_GROUP = 16


def block_inverse(block, size):
    sub = lax.broadcasted_iota(jnp.int32, (size, 128), 0)
    eye = (lax.broadcasted_iota(jnp.int32, (size, 128), 1) == sub + size).astype(jnp.float32)
    work = jnp.concatenate([block, jnp.zeros((size, 128 - size), jnp.float32)], axis=1) + eye
    done = []
    for start in range(0, size, FACTOR_GROUP):
        height = size - start
        sub = lax.broadcasted_iota(jnp.int32, (height, 128), 0)

        def row(array, index):
            return jnp.broadcast_to(array[index : index + 1, :], (height, 128))

        pivots = jnp.ones((height, 128), jnp.float32)
        columns = [
            jnp.broadcast_to(work[:, start + j : start + j + 1], (height, 128))
            for j in range(FACTOR_GROUP)
        ]
        for j in range(0, FACTOR_GROUP, 2):
            first, second = columns[j], columns[j + 1]
            a, e, b = row(first, j), row(first, j + 1), row(second, j + 1)
            det = a * b - e * e
            inverse_det, inverse_a = 1.0 / det, 1.0 / a
            ratio = jnp.where(sub > j + 1, (first * b - second * e) * inverse_det, 0.0)
            ratio = jnp.where(sub == j + 1, e * inverse_a, ratio)
            other = jnp.where(sub > j + 1, (second * a - first * e) * inverse_det, 0.0)
            pivots = jnp.where(sub == j, a, jnp.where(sub == j + 1, det * inverse_a, pivots))
            for later in range(j + 2, FACTOR_GROUP):
                column = columns[later]
                columns[later] = column - ratio * row(column, j) - other * row(column, j + 1)
            work = work - ratio * row(work, j) - other * row(work, j + 1)
        done.append(work[:FACTOR_GROUP] * lax.rsqrt(pivots[:FACTOR_GROUP]))
        work = work[FACTOR_GROUP:]
    return jnp.concatenate(done, axis=0)[:, size : 2 * size]


def inverse_factor(rows):
    step = FACTOR_BLOCK
    rows = list(rows)
    count = len(rows)

    def with_column(row, k, block):
        pieces = [row[:, q * step : (q + 1) * step] for q in range(count)]
        return jnp.concatenate(pieces[:k] + [block] + pieces[k + 1 :], axis=1)

    for k in range(count):
        inverse = block_inverse(rows[k][:, k * step : (k + 1) * step], step)
        panel = jnp.dot(inverse, rows[k], precision=HIGHEST, preferred_element_type=jnp.float32)
        rows[k] = with_column(panel, k, inverse)
        for i in range(k + 1, count):
            lower = nt_dot(rows[i][:, k * step : (k + 1) * step], inverse, HIGHEST)
            rows[i] = with_column(rows[i], k, jnp.zeros((step, step), jnp.float32)) - jnp.dot(
                lower, rows[k], precision=HIGHEST, preferred_element_type=jnp.float32
            )
    return jnp.concatenate(rows, axis=0)


def gram_kernel(parts_ref, basis_ref, copies_ref, gram_ref):
    basis = (parts_ref[0] + parts_ref[1]) + (parts_ref[2] + parts_ref[3])
    basis_ref[...] = basis
    half = basis.shape[1] // 2
    turned = basis.T
    left = jnp.dot(
        turned, basis[:, :half], precision=HIGHEST, preferred_element_type=jnp.float32
    )
    right = jnp.dot(
        turned[half:], basis[:, half:], precision=HIGHEST, preferred_element_type=jnp.float32
    )
    gram_ref[0 : 2 * half, :] = left
    gram_ref[2 * half :, :] = right
    share = half // copies_ref.shape[0]
    first = pl.multiple_of(lax.axis_index("tp") * share, share)
    for quarter in range(3):
        piece = gram_ref[pl.ds(quarter * half + first, share), :]
        copies_ref[:, quarter * share : (quarter + 1) * share, :] = jnp.broadcast_to(
            piece[None], (copies_ref.shape[0],) + piece.shape
        )


def copies_kernel(parts_ref, copies_ref):
    copies_ref[...] = jnp.broadcast_to(jnp.sum(parts_ref[...], axis=0)[None], copies_ref.shape)


def solve_kernel(blocks_ref, basis_ref, ortho_ref, *, share):
    size = basis_ref.shape[1]
    height = blocks_ref.shape[1] // 3
    upper, lower, corner = [
        jnp.concatenate(
            [blocks_ref[t, q * height : (q + 1) * height] for t in range(blocks_ref.shape[0])], axis=0
        )
        for q in range(3)
    ]
    gram = jnp.concatenate(
        [jnp.concatenate([upper, lower.T], axis=1), jnp.concatenate([lower, corner], axis=1)], axis=0
    )
    source = lax.broadcasted_iota(jnp.int32, (size, size), 0)
    target = lax.broadcasted_iota(jnp.int32, (size, size), 1)
    diagonal = jnp.where(source == target, gram, 0.0)
    scale_row = lax.rsqrt(jnp.sum(diagonal, axis=0, keepdims=True))
    scale_column = lax.rsqrt(jnp.sum(diagonal, axis=1, keepdims=True))
    gram = gram * scale_column * scale_row
    inverse = inverse_factor(
        [gram[k : k + FACTOR_BLOCK] for k in range(0, size, FACTOR_BLOCK)]
    )
    inverse = jnp.where(source >= target, inverse * scale_row, 0.0)
    ortho = nt_dot(basis_ref[...], inverse, HIGHEST).astype(jnp.bfloat16)
    rank_of = device_of(target // share, second_core()) * share + target % share
    selection = (rank_of == source).astype(jnp.bfloat16)
    ortho_ref[...] = jnp.dot(ortho, selection, preferred_element_type=jnp.float32).astype(
        jnp.bfloat16
    )


VMEM = pl.BlockSpec(memory_space=pltpu.VMEM)


def local_call(kernel, name, shapes, *operands, scratch=(), flops=0):
    size = sum(math.prod(o.shape) * o.dtype.itemsize for o in operands)
    return pl.pallas_call(
        kernel,
        out_shape=shapes,
        in_specs=[VMEM] * len(operands),
        out_specs=jax.tree.map(lambda _: VMEM, shapes),
        scratch_shapes=scratch,
        compiler_params=pltpu.CompilerParams(vmem_limit_bytes=32 << 20),
        cost_estimate=pl.CostEstimate(flops=flops, bytes_accessed=2 * size, transcendentals=0),
        name=name,
    )(*operands)


def shaped(*shape, dtype=jnp.float32):
    return jax.ShapeDtypeStruct(shape, dtype)


def exchange(blocks, groups):
    return lax.all_to_all(blocks, AXES, 0, 0, axis_index_groups=groups, tiled=True)


def spread(block, groups):
    return exchange(jnp.broadcast_to(block[None], (len(groups[0]),) + block.shape), groups)


def add_up(blocks):
    parts = [blocks[i].astype(jnp.float32) for i in range(blocks.shape[0])]
    while len(parts) > 1:
        parts = [a + b for a, b in zip(parts[::2], parts[1::2])]
    return parts[0]


def device_of(place, swapped=False):
    parity, first, second = place // 16, place // 4 % 4, place % 4
    z = jnp.where(swapped, second, first) * 2 + parity // 2
    y = jnp.where(swapped, first, second) * 2 + parity % 2
    return z * SIDE + y


def second_core():
    return lax.rem(lax.axis_index("tp"), CORES) == 1


def nt_dot(a, b, precision=None):
    return lax.dot_general(
        a, b, (((1,), (1,)), ((), ())), precision=precision, preferred_element_type=jnp.float32
    )


def halves(block):
    middle = block.shape[1] // 2
    return jnp.concatenate([block[:, :middle], block[:, middle:]], axis=0)


def split_row(row, share):
    return row // (2 * share), row // share % 2, row % share


def exact_dot(a, selection):
    high = a.astype(jnp.bfloat16)
    rest = a - high.astype(jnp.float32)
    middle = rest.astype(jnp.bfloat16)
    low = (rest - middle.astype(jnp.float32)).astype(jnp.bfloat16)
    stacked = jnp.concatenate([high, middle, low], axis=0)
    product = jnp.dot(stacked, selection, preferred_element_type=jnp.float32)
    rows = a.shape[0]
    return product[:rows] + (product[rows : 2 * rows] + product[2 * rows :])


def basis_kernel(momentum_ref, gradient_ref, factor_ref, blended_ref, basis_ref, *, share):
    blended_ref[...] = (
        momentum_ref[...].astype(jnp.float32) + gradient_ref[...].astype(jnp.float32)
    ).astype(jnp.bfloat16)
    rows = blended_ref.shape[0]
    height, half = factor_ref.shape
    rank = height // 2
    place, _, low = split_row(lax.broadcasted_iota(jnp.int32, (height, rank), 0), share)
    target = lax.broadcasted_iota(jnp.int32, (height, rank), 1)
    selection = (device_of(place) * share + low == target).astype(jnp.bfloat16)
    _, part, _ = split_row(lax.broadcasted_iota(jnp.int32, (rows, height), 1), share)
    stacked = jnp.concatenate([blended_ref[:, :half], blended_ref[:, half:]], axis=0)
    products = nt_dot(stacked, factor_ref[...])
    basis_ref[...] = exact_dot(jnp.where(part == 0, products[:rows], products[rows:]), selection)


def momentum_kernel(ortho_ref, projection_ref, blended_ref, out_ref, left_ref, *, share):
    rows = ortho_ref.shape[0]
    height, half = projection_ref.shape
    rank = height // 2
    place, part, low = split_row(lax.broadcasted_iota(jnp.int32, (rank, height), 1), share)
    source = lax.broadcasted_iota(jnp.int32, (rank, height), 0)
    selection = (place * share + low == source).astype(jnp.bfloat16)
    left = jnp.dot(ortho_ref[...], selection, preferred_element_type=jnp.float32)
    part = part[0:1]
    left = jnp.concatenate([jnp.where(part == h, left, 0.0) for h in range(2)], axis=0)
    left = left.astype(jnp.bfloat16)
    left_ref[...] = left
    carried = jnp.dot(left, projection_ref[...], preferred_element_type=jnp.float32)
    for h in range(2):
        columns = slice(h * half, (h + 1) * half)
        out_ref[:, columns] = (
            blended_ref[:, columns].astype(jnp.float32)
            - (1.0 - MOMENTUM_DECAY) * carried[h * rows : (h + 1) * rows]
        ).astype(jnp.bfloat16)


def squares_kernel(projection_ref, copies_ref):
    height, half = projection_ref.shape
    blocks = []
    for first in range(0, height, 64):
        block = jnp.zeros((64, 128), jnp.float32)
        for column in range(0, half, 128):
            piece = projection_ref[first : first + 64, column : column + 128].astype(jnp.float32)
            block = block + piece * piece
        blocks.append(block)
    sums = jnp.concatenate(blocks, axis=0)
    totals = jnp.sum(sums.T, axis=0, keepdims=True)
    copies_ref[...] = jnp.zeros(copies_ref.shape, jnp.float32)
    for copy in range(copies_ref.shape[0]):
        for piece in range(height // 128):
            copies_ref[copy, piece : piece + 1, :] = totals[0:1, piece * 128 : (piece + 1) * 128]


def swap_lines(pieces, share):
    lane = lax.broadcasted_iota(jnp.int32, pieces.shape, 1)
    count = SIDE // 2
    outer = 2 * count * share
    distance = lane // outer - lane // share % count
    result = jnp.where(distance == 0, pieces, 0.0)
    for step in range(1 - count, count):
        if step:
            moved = pltpu.roll(pieces, step * (outer - share) % 128, 1)
            result = jnp.where(distance == step, moved, result)
    return result


def update_kernel(
    left_ref, projection_ref, squares_ref, sums_ref, out_ref, factor_ref, *, share, scale
):
    height, half = projection_ref.shape
    swapped = second_core()
    first = jnp.sum(jnp.stack([squares_ref[t] for t in range(0, LINE * CORES, 2)]), axis=0)
    second = jnp.sum(jnp.stack([squares_ref[t] for t in range(1, LINE * CORES, 2)]), axis=0)
    pieces = jnp.where(swapped, second, first) + swap_lines(
        jnp.where(swapped, first, second), factor_ref.shape[0]
    )
    squares = jnp.concatenate([pieces[i : i + 1] for i in range(height // 128)], axis=1)
    squares = jnp.broadcast_to(squares, (8, height))
    place, part, low = split_row(lax.broadcasted_iota(jnp.int32, (8, height), 1), share)
    other = jnp.where(
        part == 0, pltpu.roll(squares, height - share, 1), pltpu.roll(squares, share, 1)
    )
    inverse = 1.0 / (jnp.sqrt(squares + other) + EPSILON)
    left = (left_ref[...].astype(jnp.float32) * inverse[0:1]).astype(jnp.bfloat16)
    direction = jnp.dot(left, projection_ref[...], preferred_element_type=jnp.float32)
    rows = out_ref.shape[0]
    for h in range(2):
        out_ref[:, h * half : (h + 1) * half] = (
            scale * direction[h * rows : (h + 1) * rows]
        ).astype(jnp.bfloat16)
    own_share, device = factor_ref.shape[0], lax.axis_index("fsdp")
    mine = device_of(place * (share // own_share) + low // own_share, swapped) == device
    row = lax.broadcasted_iota(jnp.int32, (8, height), 0)
    mine = mine & (part == 0) & (low % own_share == row)
    own_inverse = jnp.sum(jnp.where(mine, inverse, 0.0), axis=1, keepdims=True)
    own_line = jnp.where(swapped, lax.div(device, SIDE), lax.rem(device, SIDE))
    own = jnp.zeros(factor_ref.shape, jnp.float32)
    for block in range(share // own_share):
        rows_of_block = sums_ref[block * own_share : (block + 1) * own_share, :]
        own = jnp.where(lax.div(own_line, 2) == block, rows_of_block, own)
    factor_ref[...] = own * own_inverse[0:own_share]


def body(momentum, gradient, right_factor):
    rows, cols = momentum.shape
    share = right_factor.shape[0]
    groups, columns = SIDE * SIDE, LINE * CORES
    tiles = groups // 4
    rank = share * groups
    with jax.named_scope("factor_gather"):
        whole_factor = spread(spread(halves(right_factor), STRIDED), NEAR)
        whole_factor = whole_factor.reshape(2 * rank, cols // 2)
    with jax.named_scope("basis"):
        blended, part = local_call(
            functools.partial(basis_kernel, share=share),
            "basis_part",
            (shaped(rows, cols, dtype=jnp.bfloat16), shaped(rows, rank)),
            momentum, gradient, whole_factor,
        )
        other_core = [(i, i ^ 1) for i in range(columns)]
        parts = spread(part + lax.ppermute(part, "tp", other_core), ROW)
    with jax.named_scope("gram"):
        shape = (columns, 3 * rank // 2 // columns, rank // 2)
        basis, copies = local_call(
            gram_kernel,
            "gram_part",
            (shaped(rows, rank), shaped(*shape)),
            parts,
            scratch=[pltpu.VMEM((3 * rank // 2, rank // 2), jnp.float32)],
        )
        copies = local_call(copies_kernel, "gram_first", shaped(*shape), exchange(copies, FIRST_LINE))
        copies = local_call(copies_kernel, "gram_second", shaped(*shape), exchange(copies, SECOND_LINE))
        blocks = exchange(copies, COLUMNS)
    with jax.named_scope("solve"):
        ortho_basis = local_call(
            functools.partial(solve_kernel, share=share),
            "ortho_basis",
            shaped(rows, rank, dtype=jnp.bfloat16),
            blocks, basis,
            flops=10**9,
        )
    with jax.named_scope("projection"):
        partial = lax.dot_general(
            ortho_basis, blended, (((0,), (0,)), ((), ())), preferred_element_type=jnp.float32
        ).astype(jnp.bfloat16)
        partial = exchange(partial.reshape(4, tiles * share, cols), NEAR)
        partial = add_up(partial).astype(jnp.bfloat16)
        lines = SIDE // 2
        partial = exchange(partial.reshape(lines, lines * share, cols), SPARSE_FIRST)
        partial = spread(add_up(partial).astype(jnp.bfloat16), SPARSE_SECOND)
        sums = add_up(partial)
        strided = spread(halves(sums.astype(jnp.bfloat16)), SPARSE_FIRST)
        projection = spread(strided, NEAR).reshape(2 * rank, cols // 2)
    with jax.named_scope("norms"):
        copies = local_call(squares_kernel, "squares", shaped(columns, 8, 128), projection)
        squares = exchange(copies, COLUMNS)
    with jax.named_scope("outputs"):
        momentum_next, left = local_call(
            functools.partial(momentum_kernel, share=lines * share),
            "momentum_next",
            (shaped(rows, cols, dtype=jnp.bfloat16), shaped(2 * rows, 2 * rank, dtype=jnp.bfloat16)),
            ortho_basis, projection, blended,
            flops=8 * rows * cols * rank,
        )
        scale = math.sqrt(rows * groups * cols * columns / rank)
        update, factor_next = local_call(
            functools.partial(update_kernel, share=lines * share, scale=scale),
            "update",
            (shaped(rows, cols, dtype=jnp.bfloat16), shaped(share, cols)),
            left, projection, squares, sums,
            flops=8 * rows * cols * rank,
        )
    return (momentum_next, factor_next, update)


def solution(mesh):
    placed = P(*AXES)
    return jax.shard_map(
        body,
        mesh=mesh,
        in_specs=(placed, placed, placed),
        out_specs=(placed, placed, placed),
        check_vma=False,
    )
```

```python
import functools
import math

import jax
import jax.numpy as jnp
from jax import lax
from jax.experimental import pallas as pl
from jax.experimental.pallas import tpu as pltpu
from jax.sharding import PartitionSpec as P

EPSILON = 1e-06
MOMENTUM_DECAY = 0.95
HIGHEST = lax.Precision.HIGHEST

AXES = ("fsdp", "tp")
SIDE = 8
LINE = 4
CORES = 2


def groups_of(key, order):
    found = {}
    for index in range(SIDE * SIDE * LINE * CORES):
        fsdp, tp = divmod(index, LINE * CORES)
        place = divmod(fsdp, SIDE) + divmod(tp, CORES)
        found.setdefault(key(*place), []).append((order(*place), index))
    return [[index for _, index in sorted(group)] for group in found.values()]


def tile(place, core):
    return (place - core) % SIDE // 2


NEAR = groups_of(
    lambda z, y, x, core: (tile(z, core), tile(y, core), x, core), lambda z, y, x, core: (z % 2, y % 2)
)
STRIDED = groups_of(
    lambda z, y, x, core: (z % 2, y % 2, x, core), lambda z, y, x, core: (z // 2, y // 2)
)
SPARSE_FIRST = groups_of(
    lambda z, y, x, core: (z, y % 2, x, core) if core else (z % 2, y, x, core),
    lambda z, y, x, core: y if core else z,
)
SPARSE_SECOND = groups_of(
    lambda z, y, x, core: (z % 2, y, x, core) if core else (z, y % 2, x, core),
    lambda z, y, x, core: z if core else y,
)
FIRST_LINE = groups_of(
    lambda z, y, x, core: (y, x, core), lambda z, y, x, core: z
)
SECOND_LINE = groups_of(
    lambda z, y, x, core: (z, x, core), lambda z, y, x, core: y
)
COLUMNS = groups_of(lambda z, y, x, core: (z, y), lambda z, y, x, core: (x, core))
ROW = groups_of(lambda z, y, x, core: (z, y, core), lambda z, y, x, core: x)

FACTOR_BLOCK = 64
FACTOR_GROUP = 16


def block_inverse(block, size):
    sub = lax.broadcasted_iota(jnp.int32, (size, 128), 0)
    eye = (lax.broadcasted_iota(jnp.int32, (size, 128), 1) == sub + size).astype(jnp.float32)
    work = jnp.concatenate([block, jnp.zeros((size, 128 - size), jnp.float32)], axis=1) + eye
    done = []
    for start in range(0, size, FACTOR_GROUP):
        height = size - start
        sub = lax.broadcasted_iota(jnp.int32, (height, 128), 0)

        def row(array, index):
            return jnp.broadcast_to(array[index : index + 1, :], (height, 128))

        pivots = jnp.ones((height, 128), jnp.float32)
        columns = [
            jnp.broadcast_to(work[:, start + j : start + j + 1], (height, 128))
            for j in range(FACTOR_GROUP)
        ]
        for j in range(0, FACTOR_GROUP, 2):
            first, second = columns[j], columns[j + 1]
            a, e, b = row(first, j), row(first, j + 1), row(second, j + 1)
            det = a * b - e * e
            inverse_det, inverse_a = 1.0 / det, 1.0 / a
            ratio = jnp.where(sub > j + 1, (first * b - second * e) * inverse_det, 0.0)
            ratio = jnp.where(sub == j + 1, e * inverse_a, ratio)
            other = jnp.where(sub > j + 1, (second * a - first * e) * inverse_det, 0.0)
            pivots = jnp.where(sub == j, a, jnp.where(sub == j + 1, det * inverse_a, pivots))
            for later in range(j + 2, FACTOR_GROUP):
                column = columns[later]
                columns[later] = column - ratio * row(column, j) - other * row(column, j + 1)
            work = work - ratio * row(work, j) - other * row(work, j + 1)
        done.append(work[:FACTOR_GROUP] * lax.rsqrt(pivots[:FACTOR_GROUP]))
        work = work[FACTOR_GROUP:]
    return jnp.concatenate(done, axis=0)[:, size : 2 * size]


def inverse_factor(rows):
    step = FACTOR_BLOCK
    rows = list(rows)
    count = len(rows)

    def with_column(row, k, block):
        pieces = [row[:, q * step : (q + 1) * step] for q in range(count)]
        return jnp.concatenate(pieces[:k] + [block] + pieces[k + 1 :], axis=1)

    for k in range(count):
        inverse = block_inverse(rows[k][:, k * step : (k + 1) * step], step)
        panel = jnp.dot(inverse, rows[k], precision=HIGHEST, preferred_element_type=jnp.float32)
        rows[k] = with_column(panel, k, inverse)
        for i in range(k + 1, count):
            lower = nt_dot(rows[i][:, k * step : (k + 1) * step], inverse, HIGHEST)
            rows[i] = with_column(rows[i], k, jnp.zeros((step, step), jnp.float32)) - jnp.dot(
                lower, rows[k], precision=HIGHEST, preferred_element_type=jnp.float32
            )
    return jnp.concatenate(rows, axis=0)


def gram_kernel(parts_ref, basis_ref, copies_ref, gram_ref):
    basis = (parts_ref[0] + parts_ref[1]) + (parts_ref[2] + parts_ref[3])
    basis_ref[...] = basis
    half = basis.shape[1] // 2
    turned = basis.T
    left = jnp.dot(
        turned, basis[:, :half], precision=HIGHEST, preferred_element_type=jnp.float32
    )
    right = jnp.dot(
        turned[half:], basis[:, half:], precision=HIGHEST, preferred_element_type=jnp.float32
    )
    gram_ref[0 : 2 * half, :] = left
    gram_ref[2 * half :, :] = right
    share = half // copies_ref.shape[0]
    first = pl.multiple_of(lax.axis_index("tp") * share, share)
    for quarter in range(3):
        piece = gram_ref[pl.ds(quarter * half + first, share), :]
        copies_ref[:, quarter * share : (quarter + 1) * share, :] = jnp.broadcast_to(
            piece[None], (copies_ref.shape[0],) + piece.shape
        )


def copies_kernel(parts_ref, copies_ref):
    copies_ref[...] = jnp.broadcast_to(jnp.sum(parts_ref[...], axis=0)[None], copies_ref.shape)


def solve_kernel(blocks_ref, basis_ref, ortho_ref, *, share):
    size = basis_ref.shape[1]
    height = blocks_ref.shape[1] // 3
    upper, lower, corner = [
        jnp.concatenate(
            [blocks_ref[t, q * height : (q + 1) * height] for t in range(blocks_ref.shape[0])], axis=0
        )
        for q in range(3)
    ]
    gram = jnp.concatenate(
        [jnp.concatenate([upper, lower.T], axis=1), jnp.concatenate([lower, corner], axis=1)], axis=0
    )
    source = lax.broadcasted_iota(jnp.int32, (size, size), 0)
    target = lax.broadcasted_iota(jnp.int32, (size, size), 1)
    diagonal = jnp.where(source == target, gram, 0.0)
    scale_row = lax.rsqrt(jnp.sum(diagonal, axis=0, keepdims=True))
    scale_column = lax.rsqrt(jnp.sum(diagonal, axis=1, keepdims=True))
    gram = gram * scale_column * scale_row
    inverse = inverse_factor(
        [gram[k : k + FACTOR_BLOCK] for k in range(0, size, FACTOR_BLOCK)]
    )
    inverse = jnp.where(source >= target, inverse * scale_row, 0.0)
    ortho = nt_dot(basis_ref[...], inverse, HIGHEST).astype(jnp.bfloat16)
    rank_of = device_of(target // share, second_core()) * share + target % share
    selection = (rank_of == source).astype(jnp.bfloat16)
    ortho_ref[...] = jnp.dot(ortho, selection, preferred_element_type=jnp.float32).astype(
        jnp.bfloat16
    )


VMEM = pl.BlockSpec(memory_space=pltpu.VMEM)


def local_call(kernel, name, shapes, *operands, scratch=(), flops=0):
    size = sum(math.prod(o.shape) * o.dtype.itemsize for o in operands)
    return pl.pallas_call(
        kernel,
        out_shape=shapes,
        in_specs=[VMEM] * len(operands),
        out_specs=jax.tree.map(lambda _: VMEM, shapes),
        scratch_shapes=scratch,
        compiler_params=pltpu.CompilerParams(vmem_limit_bytes=32 << 20),
        cost_estimate=pl.CostEstimate(flops=flops, bytes_accessed=2 * size, transcendentals=0),
        name=name,
    )(*operands)


def shaped(*shape, dtype=jnp.float32):
    return jax.ShapeDtypeStruct(shape, dtype)


def exchange(blocks, groups):
    return lax.all_to_all(blocks, AXES, 0, 0, axis_index_groups=groups, tiled=True)


def spread(block, groups):
    return exchange(jnp.broadcast_to(block[None], (len(groups[0]),) + block.shape), groups)


def add_up(blocks):
    parts = [blocks[i].astype(jnp.float32) for i in range(blocks.shape[0])]
    while len(parts) > 1:
        parts = [a + b for a, b in zip(parts[::2], parts[1::2])]
    return parts[0]


def device_of(place, swapped=False):
    parity, first, second = place // 16, place // 4 % 4, place % 4
    z = jnp.where(swapped, second, first) * 2 + parity // 2
    y = jnp.where(swapped, first, second) * 2 + parity % 2
    return z * SIDE + y


def second_core():
    return lax.rem(lax.axis_index("tp"), CORES) == 1


def nt_dot(a, b, precision=None):
    return lax.dot_general(
        a, b, (((1,), (1,)), ((), ())), precision=precision, preferred_element_type=jnp.float32
    )


def halves(block):
    middle = block.shape[1] // 2
    return jnp.concatenate([block[:, :middle], block[:, middle:]], axis=0)


def split_row(row, share):
    return row // (2 * share), row // share % 2, row % share


def exact_dot(a, selection):
    high = a.astype(jnp.bfloat16)
    rest = a - high.astype(jnp.float32)
    middle = rest.astype(jnp.bfloat16)
    low = (rest - middle.astype(jnp.float32)).astype(jnp.bfloat16)
    stacked = jnp.concatenate([high, middle, low], axis=0)
    product = jnp.dot(stacked, selection, preferred_element_type=jnp.float32)
    rows = a.shape[0]
    return product[:rows] + (product[rows : 2 * rows] + product[2 * rows :])


def basis_kernel(momentum_ref, gradient_ref, factor_ref, blended_ref, basis_ref, *, share):
    blended_ref[...] = (
        momentum_ref[...].astype(jnp.float32) + gradient_ref[...].astype(jnp.float32)
    ).astype(jnp.bfloat16)
    rows = blended_ref.shape[0]
    height, half = factor_ref.shape
    rank = height // 2
    place, _, low = split_row(lax.broadcasted_iota(jnp.int32, (height, rank), 0), share)
    target = lax.broadcasted_iota(jnp.int32, (height, rank), 1)
    selection = (device_of(place) * share + low == target).astype(jnp.bfloat16)
    _, part, _ = split_row(lax.broadcasted_iota(jnp.int32, (rows, height), 1), share)
    stacked = jnp.concatenate([blended_ref[:, :half], blended_ref[:, half:]], axis=0)
    products = nt_dot(stacked, factor_ref[...])
    basis_ref[...] = exact_dot(jnp.where(part == 0, products[:rows], products[rows:]), selection)


def momentum_kernel(ortho_ref, projection_ref, blended_ref, out_ref, left_ref, *, share):
    rows = ortho_ref.shape[0]
    height, half = projection_ref.shape
    rank = height // 2
    place, part, low = split_row(lax.broadcasted_iota(jnp.int32, (rank, height), 1), share)
    source = lax.broadcasted_iota(jnp.int32, (rank, height), 0)
    selection = (place * share + low == source).astype(jnp.bfloat16)
    left = jnp.dot(ortho_ref[...], selection, preferred_element_type=jnp.float32)
    part = part[0:1]
    left = jnp.concatenate([jnp.where(part == h, left, 0.0) for h in range(2)], axis=0)
    left = left.astype(jnp.bfloat16)
    left_ref[...] = left
    carried = jnp.dot(left, projection_ref[...], preferred_element_type=jnp.float32)
    for h in range(2):
        columns = slice(h * half, (h + 1) * half)
        out_ref[:, columns] = (
            blended_ref[:, columns].astype(jnp.float32)
            - (1.0 - MOMENTUM_DECAY) * carried[h * rows : (h + 1) * rows]
        ).astype(jnp.bfloat16)


def squares_kernel(projection_ref, copies_ref):
    height, half = projection_ref.shape
    blocks = []
    for first in range(0, height, 64):
        block = jnp.zeros((64, 128), jnp.float32)
        for column in range(0, half, 128):
            piece = projection_ref[first : first + 64, column : column + 128].astype(jnp.float32)
            block = block + piece * piece
        blocks.append(block)
    sums = jnp.concatenate(blocks, axis=0)
    totals = jnp.sum(sums.T, axis=0, keepdims=True)
    copies_ref[...] = jnp.zeros(copies_ref.shape, jnp.float32)
    for copy in range(copies_ref.shape[0]):
        for piece in range(height // 128):
            copies_ref[copy, piece : piece + 1, :] = totals[0:1, piece * 128 : (piece + 1) * 128]


def swap_lines(pieces, share):
    lane = lax.broadcasted_iota(jnp.int32, pieces.shape, 1)
    count = SIDE // 2
    outer = 2 * count * share
    distance = lane // outer - lane // share % count
    result = jnp.where(distance == 0, pieces, 0.0)
    for step in range(1 - count, count):
        if step:
            moved = pltpu.roll(pieces, step * (outer - share) % 128, 1)
            result = jnp.where(distance == step, moved, result)
    return result


def update_kernel(
    left_ref, projection_ref, squares_ref, sums_ref, out_ref, factor_ref, *, share, scale
):
    height, half = projection_ref.shape
    swapped = second_core()
    first = jnp.sum(jnp.stack([squares_ref[t] for t in range(0, LINE * CORES, 2)]), axis=0)
    second = jnp.sum(jnp.stack([squares_ref[t] for t in range(1, LINE * CORES, 2)]), axis=0)
    pieces = jnp.where(swapped, second, first) + swap_lines(
        jnp.where(swapped, first, second), factor_ref.shape[0]
    )
    squares = jnp.concatenate([pieces[i : i + 1] for i in range(height // 128)], axis=1)
    squares = jnp.broadcast_to(squares, (8, height))
    place, part, low = split_row(lax.broadcasted_iota(jnp.int32, (8, height), 1), share)
    other = jnp.where(
        part == 0, pltpu.roll(squares, height - share, 1), pltpu.roll(squares, share, 1)
    )
    inverse = 1.0 / (jnp.sqrt(squares + other) + EPSILON)
    left = (left_ref[...].astype(jnp.float32) * inverse[0:1]).astype(jnp.bfloat16)
    direction = jnp.dot(left, projection_ref[...], preferred_element_type=jnp.float32)
    rows = out_ref.shape[0]
    for h in range(2):
        out_ref[:, h * half : (h + 1) * half] = (
            scale * direction[h * rows : (h + 1) * rows]
        ).astype(jnp.bfloat16)
    own_share, device = factor_ref.shape[0], lax.axis_index("fsdp")
    mine = device_of(place * (share // own_share) + low // own_share, swapped) == device
    row = lax.broadcasted_iota(jnp.int32, (8, height), 0)
    mine = mine & (part == 0) & (low % own_share == row)
    own_inverse = jnp.sum(jnp.where(mine, inverse, 0.0), axis=1, keepdims=True)
    own_line = jnp.where(swapped, lax.div(device, SIDE), lax.rem(device, SIDE))
    own = jnp.zeros(factor_ref.shape, jnp.float32)
    for block in range(share // own_share):
        rows_of_block = sums_ref[block * own_share : (block + 1) * own_share, :]
        own = jnp.where(lax.div(own_line, 2) == block, rows_of_block, own)
    factor_ref[...] = own * own_inverse[0:own_share]


def body(momentum, gradient, right_factor):
    rows, cols = momentum.shape
    share = right_factor.shape[0]
    groups, columns = SIDE * SIDE, LINE * CORES
    tiles = groups // 4
    rank = share * groups
    with jax.named_scope("factor_gather"):
        whole_factor = spread(spread(halves(right_factor), STRIDED), NEAR)
        whole_factor = whole_factor.reshape(2 * rank, cols // 2)
    with jax.named_scope("basis"):
        blended, part = local_call(
            functools.partial(basis_kernel, share=share),
            "basis_part",
            (shaped(rows, cols, dtype=jnp.bfloat16), shaped(rows, rank)),
            momentum, gradient, whole_factor,
        )
        other_core = [(i, i ^ 1) for i in range(columns)]
        parts = spread(part + lax.ppermute(part, "tp", other_core), ROW)
    with jax.named_scope("gram"):
        shape = (columns, 3 * rank // 2 // columns, rank // 2)
        basis, copies = local_call(
            gram_kernel,
            "gram_part",
            (shaped(rows, rank), shaped(*shape)),
            parts,
            scratch=[pltpu.VMEM((3 * rank // 2, rank // 2), jnp.float32)],
        )
        copies = local_call(copies_kernel, "gram_first", shaped(*shape), exchange(copies, FIRST_LINE))
        copies = local_call(copies_kernel, "gram_second", shaped(*shape), exchange(copies, SECOND_LINE))
        blocks = exchange(copies, COLUMNS)
    with jax.named_scope("solve"):
        ortho_basis = local_call(
            functools.partial(solve_kernel, share=share),
            "ortho_basis",
            shaped(rows, rank, dtype=jnp.bfloat16),
            blocks, basis,
            flops=10**9,
        )
    with jax.named_scope("projection"):
        partial = lax.dot_general(
            ortho_basis, blended, (((0,), (0,)), ((), ())), preferred_element_type=jnp.float32
        ).astype(jnp.bfloat16)
        partial = exchange(partial.reshape(4, tiles * share, cols), NEAR)
        partial = add_up(partial).astype(jnp.bfloat16)
        lines = SIDE // 2
        partial = exchange(partial.reshape(lines, lines * share, cols), SPARSE_FIRST)
        partial = spread(add_up(partial).astype(jnp.bfloat16), SPARSE_SECOND)
        sums = add_up(partial)
        strided = spread(halves(sums.astype(jnp.bfloat16)), SPARSE_FIRST)
        projection = spread(strided, NEAR).reshape(2 * rank, cols // 2)
    with jax.named_scope("norms"):
        copies = local_call(squares_kernel, "squares", shaped(columns, 8, 128), projection)
        squares = exchange(copies, COLUMNS)
    with jax.named_scope("outputs"):
        momentum_next, left = local_call(
            functools.partial(momentum_kernel, share=lines * share),
            "momentum_next",
            (shaped(rows, cols, dtype=jnp.bfloat16), shaped(2 * rows, 2 * rank, dtype=jnp.bfloat16)),
            ortho_basis, projection, blended,
            flops=8 * rows * cols * rank,
        )
        scale = math.sqrt(rows * groups * cols * columns / rank)
        update, factor_next = local_call(
            functools.partial(update_kernel, share=lines * share, scale=scale),
            "update",
            (shaped(rows, cols, dtype=jnp.bfloat16), shaped(share, cols)),
            left, projection, squares, sums,
            flops=8 * rows * cols * rank,
        )
    return (momentum_next, factor_next, update)


def solution(mesh):
    placed = P(*AXES)
    return jax.shard_map(
        body,
        mesh=mesh,
        in_specs=(placed, placed, placed),
        out_specs=(placed, placed, placed),
        check_vma=False,
    )
```
